256 devices in a mesh: tm: 8 (over z), chan: 32 (over y, x, core).
Axes of the slice: x: 4, y: 4, z: 8, core: 2. Of those that a mesh axis runs over, the one named last changes fastest.
Arguments:
- raw_traces: bfloat16 [49152, 4096], P('tm', 'chan'), may hold values from -18 to 18
Outputs:
- cross_spectra: bfloat16 [32, 2, 4096, 4096], P('tm', None, 'chan')
The draws below stay inside these ranges and needn't reach their ends.
All inputs are finite; a program needn't handle non-finite values.
Results may differ from the reference program's by a relative error of at most 0.0077.
Values may be sent and summed in bfloat16 or wider, within the bound.
A program may use at most 64 MiB of HBM per device.

```python
import math
import jax
import jax.numpy as jnp
from jax import lax

NFFT = 1024
NBINS = 32
SMOOTH = 4
BAND_START = 64
CH_DEV = 128
CHANNELS = 4096
FRAMES = 96
SAMPLES = 49152


def draw_raw_traces(key, part):
    key = jax.random.fold_in(key, 11)
    gain_key, noise_key = jax.random.split(key, 2)
    gains = jnp.exp(jax.random.uniform(gain_key, (1, CHANNELS), jnp.float32, math.log(0.1), math.log(3.0)))
    noise = jnp.clip(jax.random.normal(noise_key, (SAMPLES, CHANNELS), jnp.float32), -6.0, 6.0)
    values = gains * noise
    return values.astype(jnp.bfloat16)


def setup_inputs(seed: int = 0) -> dict:
    key_list = jax.random.split(jax.random.key(seed), 2)
    return {
        "raw_traces": draw_raw_traces(jax.random.fold_in(key_list[1], 71), 0),
    }


FLOOR_FRACTION = 0.125

def spectral_table():
    span_bins = NBINS + 2 * SMOOTH
    sample = jnp.arange(NFFT, dtype=jnp.int32)
    band_bins = BAND_START - SMOOTH + jnp.arange(span_bins, dtype=jnp.int32)
    phase_turns = sample[:, None] * band_bins[None, :] % NFFT
    angles = phase_turns.astype(jnp.float32) * (2.0 * math.pi / NFFT)
    return jnp.concatenate([jnp.cos(angles), -jnp.sin(angles)], axis=1).astype(jnp.bfloat16)

def taper():
    sample = jnp.arange(NFFT, dtype=jnp.float32)
    return 0.5 - 0.5 * jnp.cos(sample * (2.0 * math.pi / NFFT))

def whiten(spectra):
    span_bins = NBINS + 2 * SMOOTH
    real_part = spectra[:, :span_bins]
    imag_part = spectra[:, span_bins:]
    magnitude = jnp.sqrt(real_part * real_part + imag_part * imag_part)
    smoothed = magnitude[:, 0:NBINS]
    for offset in range(1, 2 * SMOOTH + 1):
        smoothed = smoothed + magnitude[:, offset:offset + NBINS]
    smoothed = smoothed / (2 * SMOOTH + 1)
    factor = 1.0 / jnp.maximum(smoothed, FLOOR_FRACTION * math.sqrt(NFFT))
    band_real = real_part[:, SMOOTH:SMOOTH + NBINS] * factor
    band_imag = imag_part[:, SMOOTH:SMOOTH + NBINS] * factor
    return jnp.stack([band_real, band_imag], axis=1).astype(jnp.bfloat16)

def block_spectra(block):
    hop_len = NFFT // 2
    width_ch = block.shape[1]
    pieces = block.reshape(FRAMES, hop_len, width_ch)
    padded = jnp.concatenate([pieces, jnp.zeros((1, hop_len, width_ch), block.dtype)], axis=0)
    frames = jnp.concatenate([padded[:-1], padded[1:]], axis=1)
    windowed = (frames.astype(jnp.float32) * taper()[None, :, None]).astype(jnp.bfloat16)
    spectra = jnp.einsum('nf,knc->kfc', spectral_table().astype(jnp.float32), windowed.astype(jnp.float32))
    return whiten(spectra)

def reference(raw_traces):
    blocks = CHANNELS // CH_DEV

    def one_block(block_index):
        block = lax.dynamic_slice_in_dim(raw_traces, block_index * CH_DEV, CH_DEV, 1)
        return block_spectra(block)
    whitened = lax.map(one_block, jnp.arange(blocks, dtype=jnp.int32))
    whitened = jnp.transpose(whitened, (1, 2, 3, 0, 4)).reshape(FRAMES, 2, NBINS, CHANNELS)

    def one_bin(bin_index):
        data = lax.dynamic_index_in_dim(whitened, bin_index, 2, keepdims=False)
        real_part = data[:, 0]
        imag_part = data[:, 1]
        real_real = jnp.dot(real_part.T, real_part, preferred_element_type=jnp.float32)
        imag_imag = jnp.dot(imag_part.T, imag_part, preferred_element_type=jnp.float32)
        imag_real = jnp.dot(imag_part.T, real_part, preferred_element_type=jnp.float32)
        real_imag = jnp.dot(real_part.T, imag_part, preferred_element_type=jnp.float32)
        return jnp.stack([(real_real + imag_imag) / FRAMES, (imag_real - real_imag) / FRAMES]).astype(jnp.bfloat16)
    return lax.map(one_bin, jnp.arange(NBINS, dtype=jnp.int32))
```

```python
import functools
import math

import jax
import jax.numpy as jnp
import numpy as np
from jax import lax
from jax.experimental import pallas as pl
from jax.experimental.pallas import tpu as pltpu
from jax.sharding import PartitionSpec as P

NFFT = 1024
HOP = NFFT // 2
NBINS = 32
SMOOTH = 4
BAND_START = 64
SPAN = NBINS + 2 * SMOOTH
FLOOR = 0.125 * math.sqrt(NFFT)
TM = 8
SIDE = 4
CORES = 2
CH = 128
PIECES = 12
FRAMES = TM * PIECES
GROUP = NBINS // TM
ROWS = 2 * PIECES
DEPTH = ROWS * TM
BATCH = GROUP // 2
MESH = pl.DeviceIdType.MESH
F32 = jnp.float32
BF16 = jnp.bfloat16


def spectral_table():
    sample = np.arange(NFFT)
    bins = BAND_START - SMOOTH + np.arange(SPAN)
    angles = (sample[:, None] * bins[None, :] % NFFT).astype(np.float64) * (2.0 * math.pi / NFFT)
    table = np.concatenate([np.cos(angles), -np.sin(angles)], axis=1).astype(np.float32)
    halves = np.concatenate([table[:HOP].T, table[HOP:].T], axis=0)
    return halves.astype(jnp.bfloat16)


def taper_half():
    sample = np.arange(HOP, dtype=np.float64)
    half = 0.5 - 0.5 * np.cos(sample * (2.0 * math.pi / NFFT))
    return np.broadcast_to(half.astype(np.float32)[:, None], (HOP, CH)).copy()


def whiten(spectra):
    real, imag = spectra[:SPAN], spectra[SPAN:]
    magnitude = jnp.sqrt(real * real + imag * imag)
    two = magnitude + pltpu.roll(magnitude, SPAN - 1, 0)
    four = two + pltpu.roll(two, SPAN - 2, 0)
    eight = four + pltpu.roll(four, SPAN - 4, 0)
    nine = eight + pltpu.roll(magnitude, SPAN - 8, 0)
    factor = 1.0 / jnp.maximum(nine * (1.0 / (2 * SMOOTH + 1)), FLOOR)
    factor = pltpu.roll(factor, SMOOTH, 0)
    return real * factor, imag * factor


def gather_kernel(
    raw_hbm, table_hbm, taper_hbm, gathered, own_t,
    raw, table, taper, spec, halo_out, halo_in, white, to_tm, from_tm,
    load_sem, halo_sem, tm_send, tm_recv, ici_send, ici_recv, sib_send, sib_recv,
):
    z = lax.axis_index("tm")
    chan = lax.axis_index("chan")
    core = lax.rem(chan, CORES)
    place = chan // CORES
    y, x = place // SIDE, lax.rem(place, SIDE)

    def chan_of(yy, xx, cc):
        return (lax.rem(yy + SIDE, SIDE) * SIDE + lax.rem(xx + SIDE, SIDE)) * CORES + cc

    def place_of(dy, dx):
        return lax.rem(y + dy + SIDE, SIDE) * SIDE + lax.rem(x + dx + SIDE, SIDE)

    sibling = chan_of(y, x, 1 - core)

    chunks = [(0, 1), (1, 3), (4, 4), (8, 4)]
    loads = [
        pltpu.make_async_copy(table_hbm, table, load_sem.at[0]),
        pltpu.make_async_copy(taper_hbm, taper, load_sem.at[1]),
    ]
    for i, (first, count) in enumerate(chunks):
        part = pl.ds(first * HOP, count * HOP)
        loads.append(pltpu.make_async_copy(raw_hbm.at[part], raw.at[part], load_sem.at[2 + i]))
    for copy in loads:
        copy.start()

    barrier = pltpu.get_barrier_semaphore()
    for d in range(1, TM):
        pl.semaphore_signal(barrier, inc=1, device_id={"tm": lax.rem(z + d, TM)}, device_id_type=MESH)
    for dy, dx in ((0, 1), (0, -1), (1, 0), (-1, 0)):
        pl.semaphore_signal(barrier, inc=1, device_id={"chan": chan_of(y + dy, x + dx, core)}, device_id_type=MESH)
    pl.semaphore_signal(barrier, inc=1, device_id={"chan": sibling}, device_id_type=MESH)

    def piece(p):
        return raw[pl.ds(p * HOP, HOP), :].astype(F32)

    for copy in loads[:3]:
        copy.wait()
    rising = taper[...]
    falling = 1.0 - rising
    halo_out[...] = jnp.dot(
        table[2 * SPAN :, :], (piece(0) * falling).astype(BF16), preferred_element_type=F32
    )
    pl.semaphore_wait(barrier, TM - 1 + 5)
    halo = pltpu.make_async_remote_copy(
        src_ref=halo_out, dst_ref=halo_in, send_sem=halo_sem.at[0], recv_sem=halo_sem.at[1],
        device_id={"tm": lax.rem(z + TM - 1, TM)}, device_id_type=MESH,
    )
    halo.start()

    waited = 1
    for pair in range(PIECES // 2):
        a, b = 2 * pair, 2 * pair + 1
        while waited < len(chunks) and b >= chunks[waited][0]:
            loads[2 + waited].wait()
            waited += 1
        one, two = piece(a), piece(b)
        up = jnp.concatenate([one * taper[...], two * taper[...]], axis=1).astype(BF16)
        first = jnp.dot(table[: 2 * SPAN, :], up, preferred_element_type=F32)
        spec[a] = first[:, :CH]
        spec[b] = first[:, CH:]
        fall = 1.0 - taper[...]
        down = jnp.concatenate([one * fall, two * fall], axis=1).astype(BF16)
        second = jnp.dot(table[2 * SPAN :, :], down, preferred_element_type=F32)
        if a > 0:
            spec[a - 1] = spec[a - 1] + second[:, :CH]
        spec[b - 1] = spec[b - 1] + second[:, CH:]

    def keep(k, spectra):
        real, imag = whiten(spectra)
        white[pl.ds(2 * k * SPAN, SPAN), :] = real
        white[pl.ds((2 * k + 1) * SPAN, SPAN), :] = imag

    for k in range(PIECES - 1):
        keep(k, spec[k])
    halo.wait_recv()
    keep(PIECES - 1, spec[PIECES - 1] + jnp.where(z == TM - 1, 0.0, halo_in[...]))

    order = (4, 3, 5, 2, 6, 1, 7)
    exchanges = []
    for h in range(2):
        for owner in range(TM):
            rows = [
                white[pl.ds(SMOOTH + owner * GROUP + h * BATCH + b, ROWS, stride=SPAN), :]
                for b in range(BATCH)
            ]
            to_tm[owner, h] = jnp.concatenate(rows, axis=0).astype(BF16)
        for i, d in enumerate(order):
            target = lax.rem(z + d, TM)
            copy = pltpu.make_async_remote_copy(
                src_ref=to_tm.at[target, h], dst_ref=from_tm.at[z, h],
                send_sem=tm_send.at[h, i], recv_sem=tm_recv.at[h, i],
                device_id={"tm": target}, device_id_type=MESH,
            )
            copy.start()
            exchanges.append(copy)
        from_tm[z, h] = to_tm[z, h]

    def unit(b, dp, dq, half=None):
        dy, dx = (dq, dp) if b % 2 == 0 else (dp, dq)
        ref = gathered.at[b, core, place_of(dy, dx)]
        return ref if half is None else ref.at[pl.ds(half * (DEPTH // 2), DEPTH // 2)]

    def neighbour(b, axis, sign):
        along_x = (axis == "p") == (b % 2 == 0)
        return chan_of(y, x + sign, core) if along_x else chan_of(y + sign, x, core)

    slots = {}
    for axis, sign in (("p", -1), ("p", 1)):
        for kind in ("whole", "half"):
            slots[(axis, sign, 0, kind)] = len(slots)
    for sign in (-1, 1):
        for dp in (0, -1, 1, 2):
            for kind in ("whole", "half"):
                slots[("q", sign, dp, kind)] = len(slots)

    def hand(b, dp, dq, axis, sign, half=None):
        kind = "whole" if half is None else "half"
        slot = slots[(axis, -sign, dp if axis == "q" else 0, kind)]
        ref = unit(b, dp, dq, half)
        pltpu.make_async_remote_copy(
            src_ref=ref, dst_ref=ref, send_sem=ici_send.at[b], recv_sem=ici_recv.at[b, slot],
            device_id={"chan": neighbour(b, axis, sign)}, device_id_type=MESH,
        ).start()

    def arrive(b, dp, dq, axis, side, half=None):
        kind = "whole" if half is None else "half"
        slot = slots[(axis, side, dp if axis == "q" else 0, kind)]
        ref = unit(b, dp, dq, half)
        pltpu.make_async_remote_copy(
            src_ref=ref, dst_ref=ref, send_sem=ici_send.at[b], recv_sem=ici_recv.at[b, slot],
            device_id={"chan": neighbour(b, axis, side)}, device_id_type=MESH,
        ).wait_recv()

    def share(b, dp, dq):
        ref = unit(b, dp, dq)
        pltpu.make_async_remote_copy(
            src_ref=ref, dst_ref=ref, send_sem=sib_send.at[b], recv_sem=sib_recv.at[b],
            device_id={"chan": sibling}, device_id_type=MESH,
        ).start()

    def own(b):
        for axis in ("p", "q"):
            for sign in (1, -1):
                hand(b, 0, 0, axis, sign)
        share(b, 0, 0)

    def first_p(b, side):
        arrive(b, side, 0, "p", side)
        hand(b, side, 0, "p", -side, half=0 if side < 0 else 1)
        hand(b, side, 0, "q", 1)
        hand(b, side, 0, "q", -1)
        share(b, side, 0)

    def second_p(b):
        arrive(b, 2, 0, "p", -1, half=0)
        arrive(b, 2, 0, "p", 1, half=1)
        hand(b, 2, 0, "q", 1)
        hand(b, 2, 0, "q", -1)
        share(b, 2, 0)

    def first_q(b, dp, side):
        arrive(b, dp, side, "q", side)
        hand(b, dp, side, "q", -side, half=0 if side < 0 else 1)
        share(b, dp, side)

    def second_q(b, dp):
        arrive(b, dp, 2, "q", -1, half=0)
        arrive(b, dp, 2, "q", 1, half=1)
        share(b, dp, 2)

    for h in range(2):
        for copy in exchanges[h * (TM - 1) : (h + 1) * (TM - 1)]:
            copy.wait_recv()
        parts = [from_tm[s, h].astype(F32) for s in range(TM)]
        for b in range(BATCH):
            whole = jnp.concatenate([part[b * ROWS : (b + 1) * ROWS] for part in parts], axis=0)
            gathered[h * BATCH + b, core, place] = whole.astype(BF16)
        for b in range(BATCH):
            own(h * BATCH + b)

    for pair in ((0, 1), (2, 3)):
        for side in (-1, 1):
            for b in pair:
                first_p(b, side)
    for pair in ((0, 1), (2, 3)):
        for side in (-1, 1):
            for b in pair:
                first_q(b, 0, side)
        for b in pair:
            second_p(b)

    parity = lax.rem(lax.broadcasted_iota(jnp.int32, (DEPTH, CH), 0), 2)
    for b in range(GROUP):
        rows = gathered[b, core, place].astype(F32)
        turned = jnp.where(parity == 0, pltpu.roll(rows, DEPTH - 1, 0), -pltpu.roll(rows, 1, 0))
        own_t[b, :CH, :] = rows.T.astype(BF16)
        own_t[b, CH:, :] = turned.T.astype(BF16)

    for pair in ((0, 1), (2, 3)):
        for dp in (-1, 1):
            for side in (-1, 1):
                for b in pair:
                    first_q(b, dp, side)
        for b in pair:
            second_q(b, 0)
    for pair in ((0, 1), (2, 3)):
        for side in (-1, 1):
            for b in pair:
                first_q(b, 2, side)
    for pair in ((0, 1), (2, 3)):
        for dp in (-1, 1):
            for b in pair:
                second_q(b, dp)
    for pair in ((0, 1), (2, 3)):
        for b in pair:
            second_q(b, 2)

    halo.wait_send()
    for copy in exchanges:
        copy.wait_send()
    for b in range(GROUP):
        sent = gathered.at[b, core, pl.ds(0, SIDE * SIDE - 1)]
        pltpu.make_async_remote_copy(
            src_ref=sent, dst_ref=sent, send_sem=ici_send.at[b], recv_sem=ici_recv.at[b, 0],
            device_id={"chan": sibling}, device_id_type=MESH,
        ).wait_send()
        shared = pltpu.make_async_remote_copy(
            src_ref=gathered.at[b, core], dst_ref=gathered.at[b, 1 - core],
            send_sem=sib_send.at[b], recv_sem=sib_recv.at[b],
            device_id={"chan": sibling}, device_id_type=MESH,
        )
        shared.wait_send()
        shared.wait_recv()


TILE = 4


def product_kernel(gathered, own_t, out, held, sems):
    steps = SIDE * SIDE // TILE
    wide = TILE * CORES * CH

    def copy_of(t):
        b, g = t // steps, lax.rem(t, steps)
        columns = pl.ds(pl.multiple_of(g * wide, wide), wide)
        return pltpu.make_async_copy(held.at[b, :, :, columns], out.at[b, :, :, columns], sems.at[t])

    def step(t, carry):
        b, g = t // steps, lax.rem(t, steps)
        for i in range(TILE):
            q = g * TILE + i
            right = jnp.concatenate([gathered[b, 0, q], gathered[b, 1, q]], axis=1)
            product = jnp.dot(own_t[b], right, preferred_element_type=F32) * (1.0 / FRAMES)
            product = product.astype(BF16)
            columns = pl.ds(pl.multiple_of(q * CORES * CH, CORES * CH), CORES * CH)
            held[b, 0, :, columns] = product[:CH]
            held[b, 1, :, columns] = product[CH:]
        copy_of(t).start()
        return carry

    lax.fori_loop(0, GROUP * steps, step, 0)

    def finish(t, carry):
        copy_of(t).wait()
        return carry

    lax.fori_loop(0, GROUP * steps, finish, 0)


def local(raw_traces):
    any_space = pl.BlockSpec(memory_space=pl.ANY)
    vmem = pl.BlockSpec(memory_space=pltpu.VMEM)
    gathered, own_t = pl.pallas_call(
        gather_kernel,
        out_shape=(
            pltpu.VMEM((GROUP, CORES, SIDE * SIDE, DEPTH, CH), BF16),
            pltpu.VMEM((GROUP, 2 * CH, DEPTH), BF16),
        ),
        in_specs=[any_space] * 3,
        out_specs=(vmem, vmem),
        scratch_shapes=[
            pltpu.VMEM((PIECES * HOP, CH), BF16),
            pltpu.VMEM((4 * SPAN, HOP), BF16),
            pltpu.VMEM((HOP, CH), F32),
            pltpu.VMEM((PIECES, 2 * SPAN, CH), F32),
            pltpu.VMEM((2 * SPAN, CH), F32),
            pltpu.VMEM((2 * SPAN, CH), F32),
            pltpu.VMEM((ROWS * SPAN, CH), F32),
            pltpu.VMEM((TM, 2, BATCH * ROWS, CH), BF16),
            pltpu.VMEM((TM, 2, BATCH * ROWS, CH), BF16),
            pltpu.SemaphoreType.DMA((6,)),
            pltpu.SemaphoreType.DMA((2,)),
            pltpu.SemaphoreType.DMA((2, TM - 1)),
            pltpu.SemaphoreType.DMA((2, TM - 1)),
            pltpu.SemaphoreType.DMA((GROUP,)),
            pltpu.SemaphoreType.DMA((GROUP, 20)),
            pltpu.SemaphoreType.DMA((GROUP,)),
            pltpu.SemaphoreType.DMA((GROUP,)),
        ],
        compiler_params=pltpu.CompilerParams(
            collective_id=0, has_side_effects=True, vmem_limit_bytes=24 * 1024 * 1024
        ),
    )(raw_traces, jnp.asarray(spectral_table()), jnp.asarray(taper_half()))
    return pl.pallas_call(
        product_kernel,
        out_shape=jax.ShapeDtypeStruct((GROUP, 2, CH, SIDE * SIDE * CORES * CH), BF16),
        in_specs=[vmem, vmem],
        out_specs=any_space,
        scratch_shapes=[
            pltpu.VMEM((GROUP, 2, CH, SIDE * SIDE * CORES * CH), BF16),
            pltpu.SemaphoreType.DMA((GROUP * SIDE * SIDE // TILE,)),
        ],
        compiler_params=pltpu.CompilerParams(vmem_limit_bytes=24 * 1024 * 1024),
    )(
        pltpu.with_memory_space_constraint(gathered, pltpu.VMEM),
        pltpu.with_memory_space_constraint(own_t, pltpu.VMEM),
    )


def solution(mesh):
    return jax.shard_map(
        local, mesh=mesh, in_specs=(P("tm", "chan"),), out_specs=P("tm", None, "chan", None), check_vma=False
    )
```

```python
import functools
import math

import jax
import jax.numpy as jnp
import numpy as np
from jax import lax
from jax.experimental import pallas as pl
from jax.experimental.pallas import tpu as pltpu
from jax.sharding import PartitionSpec as P

NFFT = 1024
HOP = NFFT // 2
NBINS = 32
SMOOTH = 4
BAND_START = 64
SPAN = NBINS + 2 * SMOOTH
FLOOR = 0.125 * math.sqrt(NFFT)
TM = 8
SIDE = 4
CORES = 2
CH = 128
PIECES = 12
FRAMES = TM * PIECES
GROUP = NBINS // TM
ROWS = 2 * PIECES
PAIR = 2 * ROWS
SIZES = (PAIR, 2 * PAIR, 2 * PAIR, 2 * PAIR, PAIR)
STARTS = (0, PAIR, 3 * PAIR, 5 * PAIR, 7 * PAIR)
UNIT = 8 * PAIR
CUTS = (32, PAIR, PAIR, PAIR, 16)
DEPTH = 5 * PAIR
MESH = pl.DeviceIdType.MESH
F32 = jnp.float32
BF16 = jnp.bfloat16


def spectral_table():
    sample = np.arange(NFFT)
    bins = BAND_START - SMOOTH + np.arange(SPAN)
    angles = (sample[:, None] * bins[None, :] % NFFT).astype(np.float64) * (2.0 * math.pi / NFFT)
    table = np.concatenate([np.cos(angles), -np.sin(angles)], axis=1).astype(np.float32)
    halves = np.concatenate([table[:HOP].T, table[HOP:].T], axis=0)
    return jnp.asarray(halves.astype(BF16))


def taper_half():
    sample = np.arange(HOP, dtype=np.float64)
    half = 0.5 - 0.5 * np.cos(sample * (2.0 * math.pi / NFFT))
    return jnp.asarray(np.broadcast_to(half.astype(np.float32)[:, None], (HOP, CH)))


def part_of(c, half=None):
    if half is None:
        return pl.ds(STARTS[c], SIZES[c])
    if half == 0:
        return pl.ds(STARTS[c], CUTS[c])
    return pl.ds(STARTS[c] + CUTS[c], SIZES[c] - CUTS[c])


def depth_of(i):
    starts = [STARTS[0]] + [STARTS[c] + i * PAIR for c in (1, 2, 3)] + [STARTS[4]]
    return [pl.ds(start, PAIR) for start in starts]


def whiten(spectra):
    real, imag = spectra[:SPAN], spectra[SPAN:]
    magnitude = jnp.sqrt(real * real + imag * imag)
    two = magnitude + pltpu.roll(magnitude, SPAN - 1, 0)
    four = two + pltpu.roll(two, SPAN - 2, 0)
    eight = four + pltpu.roll(four, SPAN - 4, 0)
    nine = eight + pltpu.roll(magnitude, SPAN - 8, 0)
    factor = 1.0 / jnp.maximum(nine * (1.0 / (2 * SMOOTH + 1)), FLOOR)
    factor = pltpu.roll(factor, SMOOTH, 0)
    return real * factor, imag * factor


def gather_kernel(
    raw_hbm, table_hbm, taper_hbm, gathered, own_t,
    raw, table, taper, spec, halo_out, halo_in, white, to_tm, from_tm,
    load_sem, halo_sem, tm_send, tm_recv, ici_send, ici_recv, sib_send, sib_recv,
):
    z = lax.axis_index("tm")
    chan = lax.axis_index("chan")
    core = lax.rem(chan, CORES)
    place = chan // CORES
    y, x = place // SIDE, lax.rem(place, SIDE)

    def chan_of(yy, xx, cc):
        return (lax.rem(yy + SIDE, SIDE) * SIDE + lax.rem(xx + SIDE, SIDE)) * CORES + cc

    sibling = chan_of(y, x, 1 - core)

    chunks = [(0, 1), (1, 3), (4, 4), (8, 4)]
    loads = [
        pltpu.make_async_copy(table_hbm, table, load_sem.at[0]),
        pltpu.make_async_copy(taper_hbm, taper, load_sem.at[1]),
    ]
    for i, (first, count) in enumerate(chunks):
        part = pl.ds(first * HOP, count * HOP)
        loads.append(pltpu.make_async_copy(raw_hbm.at[part], raw.at[part], load_sem.at[2 + i]))
    for copy in loads:
        copy.start()

    barrier = pltpu.get_barrier_semaphore()
    for d in range(1, TM):
        pl.semaphore_signal(barrier, inc=1, device_id={"tm": lax.rem(z + d, TM)}, device_id_type=MESH)
    for dy, dx in ((0, 1), (0, -1), (1, 0), (-1, 0)):
        pl.semaphore_signal(barrier, inc=1, device_id={"chan": chan_of(y + dy, x + dx, core)}, device_id_type=MESH)
    pl.semaphore_signal(barrier, inc=1, device_id={"chan": sibling}, device_id_type=MESH)

    def piece(p):
        return raw[pl.ds(p * HOP, HOP), :].astype(F32)

    for copy in loads[:3]:
        copy.wait()
    rising = taper[...]
    falling = 1.0 - rising
    halo_out[...] = jnp.dot(
        table[2 * SPAN :, :], (piece(0) * falling).astype(BF16), preferred_element_type=F32
    )
    pl.semaphore_wait(barrier, TM - 1 + 5)
    halo = pltpu.make_async_remote_copy(
        src_ref=halo_out, dst_ref=halo_in, send_sem=halo_sem.at[0], recv_sem=halo_sem.at[1],
        device_id={"tm": lax.rem(z + TM - 1, TM)}, device_id_type=MESH,
    )
    halo.start()

    waited = 1
    for pair in range(PIECES // 2):
        a, b = 2 * pair, 2 * pair + 1
        while waited < len(chunks) and b >= chunks[waited][0]:
            loads[2 + waited].wait()
            waited += 1
        one, two = piece(a), piece(b)
        up = jnp.concatenate([one * taper[...], two * taper[...]], axis=1).astype(BF16)
        first = jnp.dot(table[: 2 * SPAN, :], up, preferred_element_type=F32)
        spec[a] = first[:, :CH]
        spec[b] = first[:, CH:]
        fall = 1.0 - taper[...]
        down = jnp.concatenate([one * fall, two * fall], axis=1).astype(BF16)
        second = jnp.dot(table[2 * SPAN :, :], down, preferred_element_type=F32)
        if a > 0:
            spec[a - 1] = spec[a - 1] + second[:, :CH]
        spec[b - 1] = spec[b - 1] + second[:, CH:]

    def keep(k, spectra):
        real, imag = whiten(spectra)
        white[pl.ds(2 * k * SPAN, SPAN), :] = real
        white[pl.ds((2 * k + 1) * SPAN, SPAN), :] = imag

    for k in range(PIECES - 1):
        keep(k, spec[k])
    halo.wait_recv()
    keep(PIECES - 1, spec[PIECES - 1] + jnp.where(z == TM - 1, 0.0, halo_in[...]))

    def group_rows(owner):
        rows = [
            white[pl.ds(SMOOTH + owner * GROUP + b, ROWS, stride=SPAN), :] for b in range(GROUP)
        ]
        return jnp.concatenate(rows, axis=0)

    def lines(dp, dq, m):
        dy, dx = (dq, dp) if m == 0 else (dp, dq)
        return lax.rem(y + dy + SIDE, SIDE), lax.rem(x + dx + SIDE, SIDE)

    def unit(m, c, dp, half=None):
        yy, xx = lines(dp, 0, m)
        return gathered.at[m, core, yy, xx, part_of(c, half)]

    def line(m, c, dq, half=None):
        yy, xx = lines(0, dq, m)
        if m == 0:
            return gathered.at[m, core, yy, :, part_of(c, half)]
        return gathered.at[m, core, :, xx, part_of(c, half)]

    def neighbour(m, axis, sign):
        along_x = (axis == 0) == (m == 0)
        return chan_of(y, x + sign, core) if along_x else chan_of(y + sign, x, core)

    def copy_of(m, c, axis, side, half, ref, to):
        slot = axis * 4 + (0 if side < 0 else 1) * 2 + (0 if half is None else 1)
        return pltpu.make_async_remote_copy(
            src_ref=ref, dst_ref=ref, send_sem=ici_send.at[m, axis], recv_sem=ici_recv.at[m, c, slot],
            device_id={"chan": neighbour(m, axis, to)}, device_id_type=MESH,
        )

    def hand(m, c, axis, sign, ref, half=None):
        copy_of(m, c, axis, -sign, half, ref, sign).start()

    def arrive(m, c, axis, side, ref, half=None):
        copy_of(m, c, axis, side, half, ref, side).wait_recv()

    def share(m, c, dq):
        ref = line(m, c, dq)
        pltpu.make_async_remote_copy(
            src_ref=ref, dst_ref=ref, send_sem=sib_send.at[m], recv_sem=sib_recv.at[m],
            device_id={"chan": sibling}, device_id_type=MESH,
        ).start()

    def own(c):
        for m in range(2):
            for sign in (1, -1):
                hand(m, c, 0, sign, unit(m, c, 0))

    def first(c):
        for side in (-1, 1):
            for m in range(2):
                arrive(m, c, 0, side, unit(m, c, side))
                half = 0 if side < 0 else 1
                hand(m, c, 0, -side, unit(m, c, side, half), half)

    def second(c):
        for m in range(2):
            arrive(m, c, 0, -1, unit(m, c, 2, 0), 0)
            arrive(m, c, 0, 1, unit(m, c, 2, 1), 1)
            hand(m, c, 1, 1, line(m, c, 0))
            hand(m, c, 1, -1, line(m, c, 0))
            share(m, c, 0)

    def third(c):
        for side in (-1, 1):
            for m in range(2):
                arrive(m, c, 1, side, line(m, c, side))
                half = 0 if side < 0 else 1
                hand(m, c, 1, -side, line(m, c, side, half), half)
                share(m, c, side)

    def fourth(c):
        for m in range(2):
            arrive(m, c, 1, -1, line(m, c, 2, 0), 0)
            arrive(m, c, 1, 1, line(m, c, 2, 1), 1)
            share(m, c, 2)

    def keep_unit(c, m, rows):
        gathered[m, core, y, x, pl.ds(STARTS[c], SIZES[c]), :] = rows.astype(BF16)

    order = (1, -1, 2, -2, 3, -3, 4)
    own_rows = group_rows(z)
    for m in range(2):
        keep_unit(0, m, own_rows[m * PAIR : (m + 1) * PAIR])
    own(0)
    exchanges = {}
    for i, d in enumerate(order):
        target = lax.rem(z + d + TM, TM)
        to_tm[i] = group_rows(target).astype(BF16)
        exchanges[d] = pltpu.make_async_remote_copy(
            src_ref=to_tm.at[i], dst_ref=from_tm.at[i],
            send_sem=tm_send.at[i], recv_sem=tm_recv.at[i],
            device_id={"tm": target}, device_id_type=MESH,
        )
        exchanges[d].start()

    def receive(c):
        if c == 4:
            exchanges[4].wait_recv()
            rows = from_tm[order.index(4)]
            for m in range(2):
                keep_unit(c, m, rows[m * PAIR : (m + 1) * PAIR])
        else:
            both = []
            for d in (c, -c):
                exchanges[d].wait_recv()
                both.append(from_tm[order.index(d)].astype(F32))
            for m in range(2):
                parts = []
                for b in range(2):
                    start = (2 * m + b) * ROWS
                    parts += [rows[start : start + ROWS] for rows in both]
                keep_unit(c, m, jnp.concatenate(parts, axis=0))
        own(c)

    def transpose_own():
        row = lax.broadcasted_iota(jnp.int32, (DEPTH, CH), 0)
        for b in range(GROUP):
            m, i = b // 2, b % 2
            rows = jnp.concatenate([gathered[m, core, y, x, part, :] for part in depth_of(i)], axis=0).astype(F32)
            other = (1 - i) * ROWS
            kept = True
            for start in (0, DEPTH - PAIR):
                kept = kept & ((row < start + other) | (row >= start + other + ROWS))
            rows = jnp.where(kept, rows, 0.0)
            turned = jnp.where(lax.rem(row, 2) == 0, pltpu.roll(rows, DEPTH - 1, 0), -pltpu.roll(rows, 1, 0))
            own_t[b, :CH, :] = rows.T.astype(BF16)
            own_t[b, CH:, :] = turned.T.astype(BF16)

    receive(1)
    first(0)
    second(0)
    receive(2)
    first(1)
    second(1)
    third(0)
    receive(3)
    first(2)
    fourth(0)
    second(2)
    third(1)
    receive(4)
    first(3)
    second(3)
    transpose_own()
    fourth(1)
    third(2)
    first(4)
    second(4)
    fourth(2)
    third(3)
    fourth(3)
    third(4)
    fourth(4)

    halo.wait_send()
    for d in order:
        exchanges[d].wait_send()
    for m in range(2):
        for axis, sent in ((0, gathered.at[m, core, 0, pl.ds(0, 3)]), (1, gathered.at[m, core, pl.ds(0, 3)])):
            pltpu.make_async_remote_copy(
                src_ref=sent, dst_ref=sent, send_sem=ici_send.at[m, axis], recv_sem=ici_recv.at[m, 0, 0],
                device_id={"chan": sibling}, device_id_type=MESH,
            ).wait_send()
        shared = pltpu.make_async_remote_copy(
            src_ref=gathered.at[m, core], dst_ref=gathered.at[m, 1 - core],
            send_sem=sib_send.at[m], recv_sem=sib_recv.at[m],
            device_id={"chan": sibling}, device_id_type=MESH,
        )
        shared.wait_send()
        shared.wait_recv()


TILE = 4


def product_kernel(gathered, own_t, out, held, sems):
    steps = SIDE * SIDE // TILE
    wide = TILE * CORES * CH

    def copy_of(b, g):
        columns = pl.ds(pl.multiple_of(g * wide, wide), wide)
        return pltpu.make_async_copy(held.at[b, :, :, columns], out.at[b, :, :, columns], sems.at[b, g])

    def step(g, b):
        m, i = b // 2, b % 2
        for x in range(SIDE):
            right = jnp.concatenate(
                [jnp.concatenate([gathered[m, c, g, x, part, :] for part in depth_of(i)], axis=0) for c in range(CORES)],
                axis=1,
            )
            product = jnp.dot(own_t[b], right, preferred_element_type=F32) * (1.0 / FRAMES)
            product = product.astype(BF16)
            columns = pl.ds(pl.multiple_of(g * wide + x * CORES * CH, CORES * CH), CORES * CH)
            held[b, 0, :, columns] = product[:CH]
            held[b, 1, :, columns] = product[CH:]
        copy_of(b, g).start()

    for b in range(GROUP):
        @pl.loop(0, steps)
        def _(g):
            step(g, b)

    for b in range(GROUP):
        @pl.loop(0, steps)
        def _(g):
            copy_of(b, g).wait()


def local(raw_traces):
    any_space = pl.BlockSpec(memory_space=pl.ANY)
    vmem = pl.BlockSpec(memory_space=pltpu.VMEM)
    gathered, own_t = pl.pallas_call(
        gather_kernel,
        out_shape=(
            pltpu.VMEM((2, CORES, SIDE, SIDE, UNIT, CH), BF16),
            pltpu.VMEM((GROUP, 2 * CH, DEPTH), BF16),
        ),
        in_specs=[any_space] * 3,
        out_specs=(vmem, vmem),
        scratch_shapes=[
            pltpu.VMEM((PIECES * HOP, CH), BF16),
            pltpu.VMEM((4 * SPAN, HOP), BF16),
            pltpu.VMEM((HOP, CH), F32),
            pltpu.VMEM((PIECES, 2 * SPAN, CH), F32),
            pltpu.VMEM((2 * SPAN, CH), F32),
            pltpu.VMEM((2 * SPAN, CH), F32),
            pltpu.VMEM((ROWS * SPAN, CH), F32),
            pltpu.VMEM((TM - 1, GROUP * ROWS, CH), BF16),
            pltpu.VMEM((TM - 1, GROUP * ROWS, CH), BF16),
            pltpu.SemaphoreType.DMA((6,)),
            pltpu.SemaphoreType.DMA((2,)),
            pltpu.SemaphoreType.DMA((TM - 1,)),
            pltpu.SemaphoreType.DMA((TM - 1,)),
            pltpu.SemaphoreType.DMA((2, 2)),
            pltpu.SemaphoreType.DMA((2, 5, 8)),
            pltpu.SemaphoreType.DMA((2,)),
            pltpu.SemaphoreType.DMA((2,)),
        ],
        compiler_params=pltpu.CompilerParams(
            collective_id=0, has_side_effects=True, vmem_limit_bytes=24 * 1024 * 1024
        ),
    )(*(pltpu.with_memory_space_constraint(a, pltpu.HBM) for a in (raw_traces, spectral_table(), taper_half())))
    return pl.pallas_call(
        product_kernel,
        out_shape=jax.ShapeDtypeStruct((GROUP, 2, CH, SIDE * SIDE * CORES * CH), BF16),
        in_specs=[vmem, vmem],
        out_specs=any_space,
        scratch_shapes=[
            pltpu.VMEM((GROUP, 2, CH, SIDE * SIDE * CORES * CH), BF16),
            pltpu.SemaphoreType.DMA((GROUP, SIDE * SIDE // TILE)),
        ],
        compiler_params=pltpu.CompilerParams(vmem_limit_bytes=24 * 1024 * 1024),
    )(
        pltpu.with_memory_space_constraint(gathered, pltpu.VMEM),
        pltpu.with_memory_space_constraint(own_t, pltpu.VMEM),
    )


def solution(mesh):
    return jax.shard_map(
        local, mesh=mesh, in_specs=(P("tm", "chan"),), out_specs=P("tm", None, "chan", None), check_vma=False
    )
```

```python
import functools
import math

import jax
import jax.numpy as jnp
import numpy as np
from jax import lax
from jax.experimental import pallas as pl
from jax.experimental.pallas import tpu as pltpu
from jax.sharding import PartitionSpec as P

NFFT = 1024
HOP = NFFT // 2
NBINS = 32
SMOOTH = 4
BAND_START = 64
SPAN = NBINS + 2 * SMOOTH
FLOOR = 0.125 * math.sqrt(NFFT)
TM = 8
SIDE = 4
CORES = 2
CH = 128
PIECES = 12
FRAMES = TM * PIECES
GROUP = NBINS // TM
ROWS = 2 * PIECES
HALF = TM // 2
FULL = 2 * (PIECES - 1)
EARLY = 2 * HALF * FULL
LAST = 2 * 2 * TM
UNIT = 2 * EARLY + LAST
STARTS = (0, EARLY)
SIZES = (EARLY, EARLY + LAST)
CUT = 96
DEPTH = 2 * CUT + LAST // 2
MESH = pl.DeviceIdType.MESH
F32 = jnp.float32
BF16 = jnp.bfloat16


def spectral_table():
    sample = np.arange(NFFT)
    bins = BAND_START - SMOOTH + np.arange(SPAN)
    angles = (sample[:, None] * bins[None, :] % NFFT).astype(np.float64) * (2.0 * math.pi / NFFT)
    table = np.concatenate([np.cos(angles), -np.sin(angles)], axis=1).astype(np.float32)
    halves = np.concatenate([table[:HOP].T, table[HOP:].T], axis=0)
    return jnp.asarray(halves.astype(BF16))


def fill_taper(taper):
    step = 2.0 * math.pi / NFFT
    sample = lax.broadcasted_iota(jnp.int32, (8, CH), 0).astype(F32) * step
    cosine, sine = 0.5 * jnp.cos(sample), 0.5 * jnp.sin(sample)
    for i in range(HOP // 8):
        angle = 8 * i * step
        taper[8 * i : 8 * i + 8, :] = 0.5 - math.cos(angle) * cosine + math.sin(angle) * sine


def part_of(c, half=None):
    if half is None:
        return pl.ds(STARTS[c], SIZES[c])
    if half == 0:
        return pl.ds(STARTS[c], CUT)
    return pl.ds(STARTS[c] + CUT, SIZES[c] - CUT)


def depth_of(i):
    shift = i * (EARLY - CUT)
    return [pl.ds(shift, CUT), pl.ds(EARLY + shift, CUT), pl.ds(2 * EARLY + i * LAST // 2, LAST // 2)]


def whiten(spectra):
    real, imag = spectra[:SPAN], spectra[SPAN:]
    magnitude = jnp.sqrt(real * real + imag * imag)
    two = magnitude + pltpu.roll(magnitude, SPAN - 1, 0)
    four = two + pltpu.roll(two, SPAN - 2, 0)
    eight = four + pltpu.roll(four, SPAN - 4, 0)
    nine = eight + pltpu.roll(magnitude, SPAN - 8, 0)
    factor = 1.0 / jnp.maximum(nine * (1.0 / (2 * SMOOTH + 1)), FLOOR)
    factor = pltpu.roll(factor, SMOOTH, 0)
    return real * factor, imag * factor


def gather_kernel(
    raw_hbm, table_hbm, gathered, own_t,
    raw, table, taper, spec, halo_out, halo_in, white, to_tm, from_tm, to_last, from_last, last, stage,
    load_sem, halo_sem, tm_send, tm_recv, ici_send, ici_recv, sib_send, sib_recv,
):
    z = lax.axis_index("tm")
    chan = lax.axis_index("chan")
    core = lax.rem(chan, CORES)
    place = chan // CORES
    y, x = place // SIDE, lax.rem(place, SIDE)

    def chan_of(yy, xx, cc):
        return (lax.rem(yy + SIDE, SIDE) * SIDE + lax.rem(xx + SIDE, SIDE)) * CORES + cc

    sibling = chan_of(y, x, 1 - core)

    chunks = [(0, 1), (1, 3), (4, 4), (8, 4)]
    loads = [pltpu.make_async_copy(table_hbm, table, load_sem.at[0])]
    for i, (first, count) in enumerate(chunks):
        part = pl.ds(first * HOP, count * HOP)
        loads.append(pltpu.make_async_copy(raw_hbm.at[part], raw.at[part], load_sem.at[1 + i]))
    for copy in loads:
        copy.start()

    barrier = pltpu.get_barrier_semaphore()
    for d in range(1, TM):
        pl.semaphore_signal(barrier, inc=1, device_id={"tm": lax.rem(z + d, TM)}, device_id_type=MESH)
    for dy, dx in ((0, 1), (0, -1), (1, 0), (-1, 0)):
        pl.semaphore_signal(barrier, inc=1, device_id={"chan": chan_of(y + dy, x + dx, core)}, device_id_type=MESH)
    pl.semaphore_signal(barrier, inc=1, device_id={"chan": sibling}, device_id_type=MESH)

    def piece(p):
        return raw[pl.ds(p * HOP, HOP), :].astype(F32)

    fill_taper(taper)
    white[pl.ds(FULL * SPAN, 2 * SPAN), :] = jnp.zeros((2 * SPAN, CH), F32)
    for copy in loads[:2]:
        copy.wait()
    halo_out[...] = jnp.dot(
        table[2 * SPAN :, :], (piece(0) * (1.0 - taper[...])).astype(BF16), preferred_element_type=F32
    )

    waited = 1
    for pair in range(PIECES // 2):
        a, b = 2 * pair, 2 * pair + 1
        while waited < len(chunks) and b >= chunks[waited][0]:
            loads[1 + waited].wait()
            waited += 1
        one, two = piece(a), piece(b)
        up = jnp.concatenate([one * taper[...], two * taper[...]], axis=1).astype(BF16)
        first = jnp.dot(table[: 2 * SPAN, :], up, preferred_element_type=F32)
        spec[a] = first[:, :CH]
        spec[b] = first[:, CH:]
        fall = 1.0 - taper[...]
        down = jnp.concatenate([one * fall, two * fall], axis=1).astype(BF16)
        second = jnp.dot(table[2 * SPAN :, :], down, preferred_element_type=F32)
        if a > 0:
            spec[a - 1] = spec[a - 1] + second[:, :CH]
        spec[b - 1] = spec[b - 1] + second[:, CH:]

    pl.semaphore_wait(barrier, TM - 1 + 5)
    halo = pltpu.make_async_remote_copy(
        src_ref=halo_out, dst_ref=halo_in, send_sem=halo_sem.at[0], recv_sem=halo_sem.at[1],
        device_id={"tm": lax.rem(z + TM - 1, TM)}, device_id_type=MESH,
    )
    halo.start()

    def keep(k, spectra):
        real, imag = whiten(spectra)
        white[pl.ds(2 * k * SPAN, SPAN), :] = real
        white[pl.ds((2 * k + 1) * SPAN, SPAN), :] = imag

    for k in range(PIECES - 1):
        keep(k, spec[k])

    order = (1, -1, 2, -2, 3, -3, 4)
    sent = []

    def exchange(kind, out, into):
        for i, d in enumerate(order):
            target = lax.rem(z + d + TM, TM)
            if kind == 0:
                rows = [
                    white[pl.ds(SMOOTH + target * GROUP + b, ROWS, stride=SPAN), :] for b in range(GROUP)
                ]
            else:
                rows = [
                    white[pl.ds((FULL + part) * SPAN + SMOOTH + target * GROUP, 8), :] for part in range(2)
                ]
            out[i] = jnp.concatenate(rows, axis=0).astype(BF16)
            copy = pltpu.make_async_remote_copy(
                src_ref=out.at[i], dst_ref=into.at[z],
                send_sem=tm_send.at[kind, i], recv_sem=tm_recv.at[kind, z],
                device_id={"tm": target}, device_id_type=MESH,
            )
            copy.start()
            sent.append(copy)

    def received(kind, source, into):
        @pl.when(z != source)
        def _():
            pltpu.make_async_remote_copy(
                src_ref=into.at[source], dst_ref=into.at[source],
                send_sem=tm_send.at[kind, 0], recv_sem=tm_recv.at[kind, source],
                device_id={"tm": lax.rem(z + 1, TM)}, device_id_type=MESH,
            ).wait_recv()

    def unit(m, c, dp, dq, half=None):
        dy, dx = (dq, dp) if m == 0 else (dp, dq)
        yy, xx = lax.rem(y + dy + SIDE, SIDE), lax.rem(x + dx + SIDE, SIDE)
        return gathered.at[m, core, yy, xx, part_of(c, half)]

    def neighbour(m, axis, sign):
        along_x = (axis == "p") == (m == 0)
        return chan_of(y, x + sign, core) if along_x else chan_of(y + sign, x, core)

    slots = {}
    for side in (-1, 1):
        for kind in (None, 1):
            slots[("p", side, 0, kind)] = len(slots)
        for dp in (0, -1, 1, 2):
            for kind in (None, 1):
                slots[("q", side, dp, kind)] = len(slots)

    def copy_of(m, c, dp, dq, axis, side, half, to):
        slot = slots[(axis, side, dp if axis == "q" else 0, None if half is None else 1)]
        ref = unit(m, c, dp, dq, half)
        return pltpu.make_async_remote_copy(
            src_ref=ref, dst_ref=ref, send_sem=ici_send.at[m, 0 if axis == "p" else 1],
            recv_sem=ici_recv.at[m, c, slot],
            device_id={"chan": neighbour(m, axis, to)}, device_id_type=MESH,
        )

    def hand(m, c, dp, dq, axis, sign, half=None):
        copy_of(m, c, dp, dq, axis, -sign, half, sign).start()

    def arrive(m, c, dp, dq, axis, side, half=None):
        copy_of(m, c, dp, dq, axis, side, half, side).wait_recv()

    def share(m, c, dp, dq):
        ref = unit(m, c, dp, dq)
        pltpu.make_async_remote_copy(
            src_ref=ref, dst_ref=ref, send_sem=sib_send.at[m], recv_sem=sib_recv.at[m],
            device_id={"chan": sibling}, device_id_type=MESH,
        ).start()

    def own(c):
        for axis in ("p", "q"):
            for m in range(2):
                for sign in (1, -1):
                    hand(m, c, 0, 0, axis, sign)
        for m in range(2):
            share(m, c, 0, 0)

    def first_p(c):
        for side in (-1, 1):
            for m in range(2):
                arrive(m, c, side, 0, "p", side)
                hand(m, c, side, 0, "p", -side, half=0 if side < 0 else 1)
                hand(m, c, side, 0, "q", 1)
                hand(m, c, side, 0, "q", -1)
                share(m, c, side, 0)

    def second_p(c):
        for m in range(2):
            arrive(m, c, 2, 0, "p", -1, half=0)
            arrive(m, c, 2, 0, "p", 1, half=1)
            hand(m, c, 2, 0, "q", 1)
            hand(m, c, 2, 0, "q", -1)
            share(m, c, 2, 0)

    def first_q(c, dp):
        for side in (-1, 1):
            for m in range(2):
                arrive(m, c, dp, side, "q", side)
                hand(m, c, dp, side, "q", -side, half=0 if side < 0 else 1)
                share(m, c, dp, side)

    def second_q(c, dp):
        for m in range(2):
            arrive(m, c, dp, 2, "q", -1, half=0)
            arrive(m, c, dp, 2, "q", 1, half=1)
            share(m, c, dp, 2)

    def collect(c):
        for s in range(HALF):
            source = c * HALF + s
            received(0, source, from_tm)
            rows = from_tm[source].astype(F32)
            for b in range(GROUP):
                m, i = b // 2, b % 2
                start = (i * HALF + s) * FULL
                stage[m, start : start + FULL, :] = rows[b * ROWS : b * ROWS + FULL]
        for m in range(2):
            gathered[m, core, y, x, pl.ds(c * EARLY, EARLY), :] = stage[m].astype(BF16)

    def collect_last():
        for source in range(TM):
            received(1, source, from_last)
            last[16 * source : 16 * source + 16, :] = from_last[source].astype(F32)
        for m in range(2):
            rows = [last[pl.ds(2 * m + i, 2 * TM, stride=8), :] for i in range(2)]
            gathered[m, core, y, x, pl.ds(2 * EARLY, LAST), :] = jnp.concatenate(rows, axis=0).astype(BF16)

    def transpose_own():
        row = lax.broadcasted_iota(jnp.int32, (DEPTH, CH), 0)
        for b in range(GROUP):
            m, i = b // 2, b % 2
            rows = jnp.concatenate([gathered[m, core, y, x, part, :] for part in depth_of(i)], axis=0).astype(F32)
            other = EARLY // 2 if i == 0 else 0
            extra = CUT - EARLY // 2
            kept = True
            for start in (0, CUT):
                kept = kept & ((row < start + other) | (row >= start + other + extra))
            rows = jnp.where(kept, rows, 0.0)
            turned = jnp.where(lax.rem(row, 2) == 0, pltpu.roll(rows, DEPTH - 1, 0), -pltpu.roll(rows, 1, 0))
            own_t[b, :CH, :] = rows.T.astype(BF16)
            own_t[b, CH:, :] = turned.T.astype(BF16)

    exchange(0, to_tm, from_tm)
    from_tm[z] = jnp.concatenate(
        [white[pl.ds(SMOOTH + z * GROUP + b, ROWS, stride=SPAN), :] for b in range(GROUP)], axis=0
    ).astype(BF16)
    collect(0)
    own(0)
    halo.wait_recv()
    keep(PIECES - 1, spec[PIECES - 1] + jnp.where(z == TM - 1, 0.0, halo_in[...]))
    exchange(1, to_last, from_last)
    from_last[z] = jnp.concatenate(
        [white[pl.ds((FULL + part) * SPAN + SMOOTH + z * GROUP, 8), :] for part in range(2)], axis=0
    ).astype(BF16)
    first_p(0)
    collect(1)
    collect_last()
    own(1)
    first_q(0, 0)
    second_p(0)
    transpose_own()
    first_p(1)
    first_q(0, -1)
    first_q(0, 1)
    second_q(0, 0)
    first_q(1, 0)
    second_p(1)
    first_q(0, 2)
    second_q(0, -1)
    second_q(0, 1)
    first_q(1, -1)
    first_q(1, 1)
    second_q(1, 0)
    second_q(0, 2)
    first_q(1, 2)
    second_q(1, -1)
    second_q(1, 1)
    second_q(1, 2)

    halo.wait_send()
    for copy in sent:
        copy.wait_send()
    for m in range(2):
        for axis, all_sent in ((0, gathered.at[m, core, 0, pl.ds(0, 3)]), (1, gathered.at[m, core, pl.ds(0, 3)])):
            pltpu.make_async_remote_copy(
                src_ref=all_sent, dst_ref=all_sent, send_sem=ici_send.at[m, axis], recv_sem=ici_recv.at[m, 0, 0],
                device_id={"chan": sibling}, device_id_type=MESH,
            ).wait_send()
        shared = pltpu.make_async_remote_copy(
            src_ref=gathered.at[m, core], dst_ref=gathered.at[m, 1 - core],
            send_sem=sib_send.at[m], recv_sem=sib_recv.at[m],
            device_id={"chan": sibling}, device_id_type=MESH,
        )
        shared.wait_send()
        shared.wait_recv()


TILE = 4


def product_kernel(gathered, own_t, out, held, sems):
    steps = SIDE * SIDE // TILE
    wide = TILE * CORES * CH

    def copy_of(b, g):
        columns = pl.ds(pl.multiple_of(g * wide, wide), wide)
        return pltpu.make_async_copy(held.at[b, :, :, columns], out.at[b, :, :, columns], sems.at[b, g])

    def step(g, b):
        m, i = b // 2, b % 2
        for x in range(SIDE):
            right = jnp.concatenate(
                [jnp.concatenate([gathered[m, c, g, x, part, :] for part in depth_of(i)], axis=0) for c in range(CORES)],
                axis=1,
            )
            product = jnp.dot(own_t[b], right, preferred_element_type=F32) * (1.0 / FRAMES)
            product = product.astype(BF16)
            columns = pl.ds(pl.multiple_of(g * wide + x * CORES * CH, CORES * CH), CORES * CH)
            held[b, 0, :, columns] = product[:CH]
            held[b, 1, :, columns] = product[CH:]
        copy_of(b, g).start()

    for b in range(GROUP):
        @pl.loop(0, steps)
        def _(g):
            step(g, b)

    for b in range(GROUP):
        @pl.loop(0, steps)
        def _(g):
            copy_of(b, g).wait()


def local(raw_traces):
    any_space = pl.BlockSpec(memory_space=pl.ANY)
    vmem = pl.BlockSpec(memory_space=pltpu.VMEM)
    gathered, own_t = pl.pallas_call(
        gather_kernel,
        out_shape=(
            pltpu.VMEM((2, CORES, SIDE, SIDE, UNIT, CH), BF16),
            pltpu.VMEM((GROUP, 2 * CH, DEPTH), BF16),
        ),
        in_specs=[any_space] * 2,
        out_specs=(vmem, vmem),
        scratch_shapes=[
            pltpu.VMEM((PIECES * HOP, CH), BF16),
            pltpu.VMEM((4 * SPAN, HOP), BF16),
            pltpu.VMEM((HOP, CH), F32),
            pltpu.VMEM((PIECES, 2 * SPAN, CH), F32),
            pltpu.VMEM((2 * SPAN, CH), F32),
            pltpu.VMEM((2 * SPAN, CH), F32),
            pltpu.VMEM((ROWS * SPAN, CH), F32),
            pltpu.VMEM((TM - 1, GROUP * ROWS, CH), BF16),
            pltpu.VMEM((TM, GROUP * ROWS, CH), BF16),
            pltpu.VMEM((TM - 1, 16, CH), BF16),
            pltpu.VMEM((TM, 16, CH), BF16),
            pltpu.VMEM((16 * TM, CH), F32),
            pltpu.VMEM((2, EARLY, CH), F32),
            pltpu.SemaphoreType.DMA((5,)),
            pltpu.SemaphoreType.DMA((2,)),
            pltpu.SemaphoreType.DMA((2, TM - 1)),
            pltpu.SemaphoreType.DMA((2, TM)),
            pltpu.SemaphoreType.DMA((2, 2)),
            pltpu.SemaphoreType.DMA((2, 2, 20)),
            pltpu.SemaphoreType.DMA((2,)),
            pltpu.SemaphoreType.DMA((2,)),
        ],
        compiler_params=pltpu.CompilerParams(
            collective_id=0, has_side_effects=True, vmem_limit_bytes=24 * 1024 * 1024
        ),
    )(*(pltpu.with_memory_space_constraint(a, pltpu.HBM) for a in (raw_traces, spectral_table())))
    return pl.pallas_call(
        product_kernel,
        out_shape=jax.ShapeDtypeStruct((GROUP, 2, CH, SIDE * SIDE * CORES * CH), BF16),
        in_specs=[vmem, vmem],
        out_specs=any_space,
        scratch_shapes=[
            pltpu.VMEM((GROUP, 2, CH, SIDE * SIDE * CORES * CH), BF16),
            pltpu.SemaphoreType.DMA((GROUP, SIDE * SIDE // TILE)),
        ],
        compiler_params=pltpu.CompilerParams(vmem_limit_bytes=24 * 1024 * 1024),
    )(
        pltpu.with_memory_space_constraint(gathered, pltpu.VMEM),
        pltpu.with_memory_space_constraint(own_t, pltpu.VMEM),
    )


def solution(mesh):
    return jax.shard_map(
        local, mesh=mesh, in_specs=(P("tm", "chan"),), out_specs=P("tm", None, "chan", None), check_vma=False
    )
```

```python
import functools
import math

import jax
import jax.numpy as jnp
import numpy as np
from jax import lax
from jax.experimental import pallas as pl
from jax.experimental.pallas import tpu as pltpu
from jax.sharding import PartitionSpec as P

NFFT = 1024
HOP = NFFT // 2
NBINS = 32
SMOOTH = 4
BAND_START = 64
SPAN = NBINS + 2 * SMOOTH
FLOOR = 0.125 * math.sqrt(NFFT)
TM = 8
SIDE = 4
CORES = 2
CH = 128
PIECES = 12
FRAMES = TM * PIECES
GROUP = NBINS // TM
ROWS = 2 * PIECES
PARTS = 3
PART = ROWS // PARTS
LINES = TM * PART
CHUNK = 2 * LINES
UNIT = PARTS * CHUNK
DEPTH = PARTS * LINES
STRAIGHT = (False, False, False)
PLAN = ((0, 0), (1, 0), (2, 0), (0, 1), (1, 1), (2, 1), (0, 2), (1, 2), (0, 3), (2, 2), (1, 3), (2, 3), (0, 4), (1, 4), (2, 4))
MESH = pl.DeviceIdType.MESH
F32 = jnp.float32
BF16 = jnp.bfloat16


def spectral_table():
    sample = np.arange(NFFT)
    bins = BAND_START - SMOOTH + np.arange(SPAN)
    angles = (sample[:, None] * bins[None, :] % NFFT).astype(np.float64) * (2.0 * math.pi / NFFT)
    table = np.concatenate([np.cos(angles), -np.sin(angles)], axis=1).astype(np.float32)
    halves = np.concatenate([table[:HOP].T, table[HOP:].T], axis=0)
    return jnp.asarray(halves.astype(BF16))


def fill_taper(taper):
    step = 2.0 * math.pi / NFFT
    sample = lax.broadcasted_iota(jnp.int32, (8, CH), 0).astype(F32) * step
    cosine, sine = 0.5 * jnp.cos(sample), 0.5 * jnp.sin(sample)
    for i in range(HOP // 8):
        angle = 8 * i * step
        taper[8 * i : 8 * i + 8, :] = 0.5 - math.cos(angle) * cosine + math.sin(angle) * sine


def part_of(c, half=None):
    if half is None:
        return pl.ds(c * CHUNK, CHUNK)
    return pl.ds(c * CHUNK + half * LINES, LINES)


def depth_of(i):
    return [pl.ds(c * CHUNK + i * LINES, LINES) for c in range(PARTS)]


def whiten(spectra):
    real, imag = spectra[:SPAN], spectra[SPAN:]
    magnitude = jnp.sqrt(real * real + imag * imag)
    two = magnitude + pltpu.roll(magnitude, SPAN - 1, 0)
    four = two + pltpu.roll(two, SPAN - 2, 0)
    eight = four + pltpu.roll(four, SPAN - 4, 0)
    nine = eight + pltpu.roll(magnitude, SPAN - 8, 0)
    factor = 1.0 / jnp.maximum(nine * (1.0 / (2 * SMOOTH + 1)), FLOOR)
    factor = pltpu.roll(factor, SMOOTH, 0)
    return real * factor, imag * factor


def gather_kernel(
    raw_hbm, table_hbm, gathered, own_t,
    raw, table, taper, spec, halo_out, halo_in, white, to_tm, from_tm,
    load_sem, halo_sem, tm_send, tm_recv, ici_send, ici_recv, sib_send, sib_recv,
):
    z = lax.axis_index("tm")
    chan = lax.axis_index("chan")
    core = lax.rem(chan, CORES)
    place = chan // CORES
    y, x = place // SIDE, lax.rem(place, SIDE)

    def chan_of(yy, xx, cc):
        return (lax.rem(yy + SIDE, SIDE) * SIDE + lax.rem(xx + SIDE, SIDE)) * CORES + cc

    sibling = chan_of(y, x, 1 - core)

    chunks = [(0, 2), (2, 2), (4, 2), (6, 2), (8, 4)]
    loads = [pltpu.make_async_copy(table_hbm, table, load_sem.at[0])]
    for i, (first, count) in enumerate(chunks):
        part = pl.ds(first * HOP, count * HOP)
        loads.append(pltpu.make_async_copy(raw_hbm.at[part], raw.at[part], load_sem.at[1 + i]))
    for copy in loads:
        copy.start()

    barrier = pltpu.get_barrier_semaphore()
    for d in range(1, TM):
        pl.semaphore_signal(barrier, inc=1, device_id={"tm": lax.rem(z + d, TM)}, device_id_type=MESH)
    for dy, dx in ((0, 1), (0, -1), (1, 0), (-1, 0), (0, 2), (2, 0)):
        pl.semaphore_signal(barrier, inc=1, device_id={"chan": chan_of(y + dy, x + dx, core)}, device_id_type=MESH)
    pl.semaphore_signal(barrier, inc=1, device_id={"chan": sibling}, device_id_type=MESH)

    def piece(p):
        return raw[pl.ds(p * HOP, HOP), :].astype(F32)

    fill_taper(taper)
    loads[0].wait()
    loads[1].wait()
    halo_out[...] = jnp.dot(
        table[2 * SPAN :, :], (piece(0) * (1.0 - taper[...])).astype(BF16), preferred_element_type=F32
    )
    halo = pltpu.make_async_remote_copy(
        src_ref=halo_out, dst_ref=halo_in, send_sem=halo_sem.at[0], recv_sem=halo_sem.at[1],
        device_id={"tm": lax.rem(z + TM - 1, TM)}, device_id_type=MESH,
    )

    def enter():
        pl.semaphore_wait(barrier, TM - 1 + 7)
        halo.start()

    middle = (z >= 3) & (z <= 6)
    pl.when(middle)(enter)

    def keep(k, spectra):
        real, imag = whiten(spectra)
        white[pl.ds(2 * k * SPAN, SPAN), :] = real
        white[pl.ds((2 * k + 1) * SPAN, SPAN), :] = imag

    def transform(pair):
        a, b = 2 * pair, 2 * pair + 1
        one, two = piece(a), piece(b)
        up = jnp.concatenate([one * taper[...], two * taper[...]], axis=1).astype(BF16)
        first = jnp.dot(table[: 2 * SPAN, :], up, preferred_element_type=F32)
        spec[a] = first[:, :CH]
        spec[b] = first[:, CH:]
        fall = 1.0 - taper[...]
        down = jnp.concatenate([one * fall, two * fall], axis=1).astype(BF16)
        second = jnp.dot(table[2 * SPAN :, :], down, preferred_element_type=F32)
        if a > 0:
            spec[a - 1] = spec[a - 1] + second[:, :CH]
        spec[b - 1] = spec[b - 1] + second[:, CH:]

    order = (1, -1, 2, -2, 3, -3, 4)
    sent = []

    def rows_for(owner, c):
        rows = [
            white[pl.ds(c * PART * SPAN + SMOOTH + owner * GROUP + b, PART, stride=SPAN), :] for b in range(GROUP)
        ]
        return jnp.concatenate(rows, axis=0).astype(BF16)

    def exchange(c):
        for i, d in enumerate(order):
            target = lax.rem(z + d + TM, TM)
            to_tm[c, i] = rows_for(target, c)
            copy = pltpu.make_async_remote_copy(
                src_ref=to_tm.at[c, i], dst_ref=from_tm.at[c, z],
                send_sem=tm_send.at[c, i], recv_sem=tm_recv.at[c, z],
                device_id={"tm": target}, device_id_type=MESH,
            )
            copy.start()
            sent.append(copy)
        from_tm[c, z] = rows_for(z, c)

    def collect(c):
        for source in range(TM):
            @pl.when(z != source)
            def _():
                pltpu.make_async_remote_copy(
                    src_ref=from_tm.at[c, source], dst_ref=from_tm.at[c, source],
                    send_sem=tm_send.at[c, 0], recv_sem=tm_recv.at[c, source],
                    device_id={"tm": lax.rem(z + 1, TM)}, device_id_type=MESH,
                ).wait_recv()
        rows = [from_tm[c, source].astype(F32) for source in range(TM)]
        for b in range(GROUP):
            m, i = b // 2, b % 2
            whole = jnp.concatenate([part[b * PART : (b + 1) * PART] for part in rows], axis=0)
            gathered[m, core, y, x, pl.ds(c * CHUNK + i * LINES, LINES), :] = whole.astype(BF16)

    frames = PIECES // PARTS
    done = 0
    for pair in range(PIECES // 2):
        a, b = 2 * pair, 2 * pair + 1
        if 0 < pair < len(chunks):
            loads[1 + pair].wait()
        transform(pair)
        for c in range(PARTS - 1):
            if b - 1 >= (c + 1) * frames - 1 > a - 2:
                for k in range(c * frames, (c + 1) * frames):
                    keep(k, spec[k])
                if c == 0:
                    pl.when(jnp.logical_not(middle))(enter)
                exchange(c)
    for k in range((PARTS - 1) * frames, PIECES - 1):
        keep(k, spec[k])
    halo.wait_recv()
    keep(PIECES - 1, spec[PIECES - 1] + jnp.where(z == TM - 1, 0.0, halo_in[...]))
    exchange(PARTS - 1)

    def unit(m, c, dp, dq, half=None):
        dy, dx = (dq, dp) if m == 0 else (dp, dq)
        yy, xx = lax.rem(y + dy + SIDE, SIDE), lax.rem(x + dx + SIDE, SIDE)
        return gathered.at[m, core, yy, xx, part_of(c, half)]

    def neighbour(m, axis, sign):
        along_x = (axis == "p") == (m == 0)
        return chan_of(y, x + sign, core) if along_x else chan_of(y + sign, x, core)

    slots = {}
    for side in (-1, 1):
        for dp in (0, -1, 1, 2):
            for kind in (None, 1):
                slots[("q", side, dp, kind)] = len(slots)
    for side in (-1, 1, 2):
        slots[("p", side, 0, None)] = len(slots)
    for dp in (0, -1, 1, 2):
        slots[("q", 2, dp, None)] = len(slots)

    def copy_of(m, c, dp, dq, axis, side, half, to):
        slot = slots[(axis, side, dp if axis == "q" else 0, None if half is None else 1)]
        ref = unit(m, c, dp, dq, half)
        return pltpu.make_async_remote_copy(
            src_ref=ref, dst_ref=ref, send_sem=ici_send.at[m, 0 if axis == "p" else 1],
            recv_sem=ici_recv.at[m, c, slot],
            device_id={"chan": neighbour(m, axis, to)}, device_id_type=MESH,
        )

    def hand(m, c, dp, dq, axis, sign, half=None):
        copy_of(m, c, dp, dq, axis, sign if sign == 2 else -sign, half, sign).start()

    def arrive(m, c, dp, dq, axis, side, half=None):
        copy_of(m, c, dp, dq, axis, side, half, side).wait_recv()

    def share(m, c, dp, dq):
        ref = unit(m, c, dp, dq)
        pltpu.make_async_remote_copy(
            src_ref=ref, dst_ref=ref, send_sem=sib_send.at[m], recv_sem=sib_recv.at[m],
            device_id={"chan": sibling}, device_id_type=MESH,
        ).start()

    def own(c):
        for m in range(2):
            for sign in (2, 1, -1):
                hand(m, c, 0, 0, "p", sign)
        for m in range(2):
            to_q(m, c, 0)
        for m in range(2):
            share(m, c, 0, 0)

    def to_q(m, c, dp):
        for sign in (2, 1, -1) if STRAIGHT[c] else (1, -1):
            hand(m, c, dp, 0, "q", sign)

    def across(c, dp):
        for m in range(2):
            arrive(m, c, dp, 0, "p", dp)
            to_q(m, c, dp)
            share(m, c, dp, 0)

    def first_q(c, dp):
        for side in (-1, 1):
            for m in range(2):
                arrive(m, c, dp, side, "q", side)
                if not STRAIGHT[c]:
                    hand(m, c, dp, side, "q", -side, half=0 if side < 0 else 1)
                share(m, c, dp, side)

    def second_q(c, dp):
        for m in range(2):
            if STRAIGHT[c]:
                arrive(m, c, dp, 2, "q", 2)
            else:
                arrive(m, c, dp, 2, "q", -1, half=0)
                arrive(m, c, dp, 2, "q", 1, half=1)
            share(m, c, dp, 2)

    def stage(c, k):
        if k == 0:
            collect(c)
            own(c)
        elif k == 1:
            for dp in (-1, 1, 2):
                across(c, dp)
        elif k == 2:
            first_q(c, 0)
        elif k == 3:
            for dp in (-1, 1, 2):
                first_q(c, dp)
        else:
            for dp in (0, -1, 1, 2):
                second_q(c, dp)

    def transpose_own():
        row = lax.broadcasted_iota(jnp.int32, (DEPTH, CH), 0)
        for b in range(GROUP):
            m, i = b // 2, b % 2
            rows = jnp.concatenate([gathered[m, core, y, x, part, :] for part in depth_of(i)], axis=0).astype(F32)
            turned = jnp.where(lax.rem(row, 2) == 0, pltpu.roll(rows, DEPTH - 1, 0), -pltpu.roll(rows, 1, 0))
            own_t[b, :CH, :] = rows.T.astype(BF16)
            own_t[b, CH:, :] = turned.T.astype(BF16)

    for c, k in PLAN:
        stage(c, k)
        if (c, k) == (0, 4):
            transpose_own()

    halo.wait_send()
    for copy in sent:
        copy.wait_send()
    for m in range(2):
        for axis, all_sent in ((0, gathered.at[m, core, 0, pl.ds(0, 3)]), (1, gathered.at[m, core, pl.ds(0, 3)])):
            pltpu.make_async_remote_copy(
                src_ref=all_sent, dst_ref=all_sent, send_sem=ici_send.at[m, axis], recv_sem=ici_recv.at[m, 0, 0],
                device_id={"chan": sibling}, device_id_type=MESH,
            ).wait_send()
        shared = pltpu.make_async_remote_copy(
            src_ref=gathered.at[m, core], dst_ref=gathered.at[m, 1 - core],
            send_sem=sib_send.at[m], recv_sem=sib_recv.at[m],
            device_id={"chan": sibling}, device_id_type=MESH,
        )
        shared.wait_send()
        shared.wait_recv()


TILE = 4


def product_kernel(gathered, own_t, out, held, sems):
    steps = SIDE * SIDE // TILE
    wide = TILE * CORES * CH

    def copy_of(b, g):
        columns = pl.ds(pl.multiple_of(g * wide, wide), wide)
        return pltpu.make_async_copy(held.at[b, :, :, columns], out.at[b, :, :, columns], sems.at[b, g])

    def step(g, b):
        m, i = b // 2, b % 2
        for x in range(SIDE):
            right = jnp.concatenate(
                [jnp.concatenate([gathered[m, c, g, x, part, :] for part in depth_of(i)], axis=0) for c in range(CORES)],
                axis=1,
            )
            product = jnp.dot(own_t[b], right, preferred_element_type=F32) * (1.0 / FRAMES)
            product = product.astype(BF16)
            columns = pl.ds(pl.multiple_of(g * wide + x * CORES * CH, CORES * CH), CORES * CH)
            held[b, 0, :, columns] = product[:CH]
            held[b, 1, :, columns] = product[CH:]
        copy_of(b, g).start()

    for b in range(GROUP):
        @pl.loop(0, steps)
        def _(g):
            step(g, b)

    for b in range(GROUP):
        @pl.loop(0, steps)
        def _(g):
            copy_of(b, g).wait()


def local(raw_traces):
    any_space = pl.BlockSpec(memory_space=pl.ANY)
    vmem = pl.BlockSpec(memory_space=pltpu.VMEM)
    gathered, own_t = pl.pallas_call(
        gather_kernel,
        out_shape=(
            pltpu.VMEM((2, CORES, SIDE, SIDE, UNIT, CH), BF16),
            pltpu.VMEM((GROUP, 2 * CH, DEPTH), BF16),
        ),
        in_specs=[any_space] * 2,
        out_specs=(vmem, vmem),
        scratch_shapes=[
            pltpu.VMEM((PIECES * HOP, CH), BF16),
            pltpu.VMEM((4 * SPAN, HOP), BF16),
            pltpu.VMEM((HOP, CH), F32),
            pltpu.VMEM((PIECES, 2 * SPAN, CH), F32),
            pltpu.VMEM((2 * SPAN, CH), F32),
            pltpu.VMEM((2 * SPAN, CH), F32),
            pltpu.VMEM((ROWS * SPAN, CH), F32),
            pltpu.VMEM((PARTS, TM - 1, GROUP * PART, CH), BF16),
            pltpu.VMEM((PARTS, TM, GROUP * PART, CH), BF16),
            pltpu.SemaphoreType.DMA((6,)),
            pltpu.SemaphoreType.DMA((2,)),
            pltpu.SemaphoreType.DMA((PARTS, TM - 1)),
            pltpu.SemaphoreType.DMA((PARTS, TM)),
            pltpu.SemaphoreType.DMA((2, 2)),
            pltpu.SemaphoreType.DMA((2, PARTS, 23)),
            pltpu.SemaphoreType.DMA((2,)),
            pltpu.SemaphoreType.DMA((2,)),
        ],
        compiler_params=pltpu.CompilerParams(
            collective_id=0, has_side_effects=True, vmem_limit_bytes=24 * 1024 * 1024
        ),
    )(*(pltpu.with_memory_space_constraint(a, pltpu.HBM) for a in (raw_traces, spectral_table())))
    return pl.pallas_call(
        product_kernel,
        out_shape=jax.ShapeDtypeStruct((GROUP, 2, CH, SIDE * SIDE * CORES * CH), BF16),
        in_specs=[vmem, vmem],
        out_specs=any_space,
        scratch_shapes=[
            pltpu.VMEM((GROUP, 2, CH, SIDE * SIDE * CORES * CH), BF16),
            pltpu.SemaphoreType.DMA((GROUP, SIDE * SIDE // TILE)),
        ],
        compiler_params=pltpu.CompilerParams(vmem_limit_bytes=24 * 1024 * 1024),
    )(
        pltpu.with_memory_space_constraint(gathered, pltpu.VMEM),
        pltpu.with_memory_space_constraint(own_t, pltpu.VMEM),
    )


def solution(mesh):
    return jax.shard_map(
        local, mesh=mesh, in_specs=(P("tm", "chan"),), out_specs=P("tm", None, "chan", None), check_vma=False
    )
```

```python
import functools
import math

import jax
import jax.numpy as jnp
import numpy as np
from jax import lax
from jax.experimental import pallas as pl
from jax.experimental.pallas import tpu as pltpu
from jax.sharding import PartitionSpec as P

NFFT = 1024
HOP = NFFT // 2
NBINS = 32
SMOOTH = 4
BAND_START = 64
SPAN = NBINS + 2 * SMOOTH
FLOOR = 0.125 * math.sqrt(NFFT)
TM = 8
SIDE = 4
CORES = 2
CH = 128
PIECES = 12
FRAMES = TM * PIECES
GROUP = NBINS // TM
ROWS = 2 * PIECES
PARTS = 3
PART = ROWS // PARTS
LINES = TM * PART
CHUNK = 2 * LINES
UNIT = PARTS * CHUNK
DEPTH = PARTS * LINES
STRAIGHT = (False, False, False)
PLAN = ((0, 0), (1, 0), (2, 0), (0, 1), (1, 1), (2, 1), (0, 2), (1, 2), (0, 3), (2, 2), (1, 3), (2, 3), (0, 4), (1, 4), (2, 4))
MESH = pl.DeviceIdType.MESH
F32 = jnp.float32
BF16 = jnp.bfloat16


def spectral_table():
    sample = np.arange(NFFT)
    bins = BAND_START - SMOOTH + np.arange(SPAN)
    angles = (sample[:, None] * bins[None, :] % NFFT).astype(np.float64) * (2.0 * math.pi / NFFT)
    table = np.concatenate([np.cos(angles), -np.sin(angles)], axis=1).astype(np.float32)
    halves = np.concatenate([table[:HOP].T, table[HOP:].T], axis=0)
    return jnp.asarray(halves.astype(BF16))


def fill_taper(taper):
    step = 2.0 * math.pi / NFFT
    sample = lax.broadcasted_iota(jnp.int32, (8, CH), 0).astype(F32) * step
    cosine, sine = 0.5 * jnp.cos(sample), 0.5 * jnp.sin(sample)
    for i in range(HOP // 8):
        angle = 8 * i * step
        taper[8 * i : 8 * i + 8, :] = 0.5 - math.cos(angle) * cosine + math.sin(angle) * sine


def part_of(c, half=None):
    if half is None:
        return pl.ds(c * CHUNK, CHUNK)
    return pl.ds(c * CHUNK + half * LINES, LINES)


def depth_of(i):
    return [pl.ds(c * CHUNK + i * LINES, LINES) for c in range(PARTS)]


def whiten(spectra):
    real, imag = spectra[:SPAN], spectra[SPAN:]
    magnitude = jnp.sqrt(real * real + imag * imag)
    two = magnitude + pltpu.roll(magnitude, SPAN - 1, 0)
    four = two + pltpu.roll(two, SPAN - 2, 0)
    eight = four + pltpu.roll(four, SPAN - 4, 0)
    nine = eight + pltpu.roll(magnitude, SPAN - 8, 0)
    factor = 1.0 / jnp.maximum(nine * (1.0 / (2 * SMOOTH + 1)), FLOOR)
    factor = pltpu.roll(factor, SMOOTH, 0)
    return real * factor, imag * factor


def gather_kernel(
    raw_hbm, table_hbm, gathered, own_t,
    raw, table, taper, spec, halo_out, halo_in, white, to_tm, from_tm,
    load_sem, halo_sem, tm_send, tm_recv, ici_send, ici_recv, sib_send, sib_recv,
):
    z = lax.axis_index("tm")
    chan = lax.axis_index("chan")
    core = lax.rem(chan, CORES)
    place = chan // CORES
    y, x = place // SIDE, lax.rem(place, SIDE)

    def chan_of(yy, xx, cc):
        return (lax.rem(yy + SIDE, SIDE) * SIDE + lax.rem(xx + SIDE, SIDE)) * CORES + cc

    sibling = chan_of(y, x, 1 - core)

    chunks = [(0, 2), (2, 2), (4, 2), (6, 2), (8, 4)]
    loads = [pltpu.make_async_copy(table_hbm, table, load_sem.at[0])]
    for i, (first, count) in enumerate(chunks):
        part = pl.ds(first * HOP, count * HOP)
        loads.append(pltpu.make_async_copy(raw_hbm.at[part], raw.at[part], load_sem.at[1 + i]))
    for copy in loads:
        copy.start()

    barrier = pltpu.get_barrier_semaphore()
    for d in range(1, TM):
        pl.semaphore_signal(barrier, inc=1, device_id={"tm": lax.rem(z + d, TM)}, device_id_type=MESH)
    for dy, dx in ((0, 1), (0, -1), (1, 0), (-1, 0), (0, 2), (2, 0)):
        pl.semaphore_signal(barrier, inc=1, device_id={"chan": chan_of(y + dy, x + dx, core)}, device_id_type=MESH)
    pl.semaphore_signal(barrier, inc=1, device_id={"chan": sibling}, device_id_type=MESH)

    def piece(p):
        return raw[pl.ds(p * HOP, HOP), :].astype(F32)

    fill_taper(taper)
    loads[0].wait()
    loads[1].wait()
    halo_out[...] = jnp.dot(
        table[2 * SPAN :, :], (piece(0) * (1.0 - taper[...])).astype(BF16), preferred_element_type=F32
    )
    halo = pltpu.make_async_remote_copy(
        src_ref=halo_out, dst_ref=halo_in, send_sem=halo_sem.at[0], recv_sem=halo_sem.at[1],
        device_id={"tm": lax.rem(z + TM - 1, TM)}, device_id_type=MESH,
    )

    def enter():
        pl.semaphore_wait(barrier, TM - 1 + 7)
        halo.start()

    middle = (z >= 3) & (z <= 6)
    pl.when(middle)(enter)

    def keep(k, spectra):
        real, imag = whiten(spectra)
        white[pl.ds(2 * k * SPAN, SPAN), :] = real
        white[pl.ds((2 * k + 1) * SPAN, SPAN), :] = imag

    def transform(pair):
        a, b = 2 * pair, 2 * pair + 1
        one, two = piece(a), piece(b)
        up = jnp.concatenate([one * taper[...], two * taper[...]], axis=1).astype(BF16)
        first = jnp.dot(table[: 2 * SPAN, :], up, preferred_element_type=F32)
        spec[a] = first[:, :CH]
        spec[b] = first[:, CH:]
        fall = 1.0 - taper[...]
        down = jnp.concatenate([one * fall, two * fall], axis=1).astype(BF16)
        second = jnp.dot(table[2 * SPAN :, :], down, preferred_element_type=F32)
        if a > 0:
            spec[a - 1] = spec[a - 1] + second[:, :CH]
        spec[b - 1] = spec[b - 1] + second[:, CH:]

    order = (1, -1, 2, -2, 3, -3, 4)
    sent = []

    def rows_for(owner, c):
        rows = [
            white[pl.ds(c * PART * SPAN + SMOOTH + owner * GROUP + b, PART, stride=SPAN), :] for b in range(GROUP)
        ]
        return jnp.concatenate(rows, axis=0).astype(BF16)

    def exchange(c):
        for i, d in enumerate(order):
            target = lax.rem(z + d + TM, TM)
            to_tm[c, i] = rows_for(target, c)
            copy = pltpu.make_async_remote_copy(
                src_ref=to_tm.at[c, i], dst_ref=from_tm.at[c, z],
                send_sem=tm_send.at[c, i], recv_sem=tm_recv.at[c, z],
                device_id={"tm": target}, device_id_type=MESH,
            )
            copy.start()
            sent.append(copy)
        from_tm[c, z] = rows_for(z, c)

    def collect(c):
        for source in range(TM):
            @pl.when(z != source)
            def _():
                pltpu.make_async_remote_copy(
                    src_ref=from_tm.at[c, source], dst_ref=from_tm.at[c, source],
                    send_sem=tm_send.at[c, 0], recv_sem=tm_recv.at[c, source],
                    device_id={"tm": lax.rem(z + 1, TM)}, device_id_type=MESH,
                ).wait_recv()
        rows = [from_tm[c, source].astype(F32) for source in range(TM)]
        for b in range(GROUP):
            m, i = b // 2, b % 2
            whole = jnp.concatenate([part[b * PART : (b + 1) * PART] for part in rows], axis=0)
            gathered[m, core, y, x, pl.ds(c * CHUNK + i * LINES, LINES), :] = whole.astype(BF16)

    frames = PIECES // PARTS
    done = 0
    for pair in range(PIECES // 2):
        a, b = 2 * pair, 2 * pair + 1
        if 0 < pair < len(chunks):
            loads[1 + pair].wait()
        transform(pair)
        for c in range(PARTS - 1):
            if b - 1 >= (c + 1) * frames - 1 > a - 2:
                for k in range(c * frames, (c + 1) * frames):
                    keep(k, spec[k])
                if c == 0:
                    pl.when(jnp.logical_not(middle))(enter)
                exchange(c)
    for k in range((PARTS - 1) * frames, PIECES - 1):
        keep(k, spec[k])
    halo.wait_recv()
    keep(PIECES - 1, spec[PIECES - 1] + jnp.where(z == TM - 1, 0.0, halo_in[...]))
    exchange(PARTS - 1)

    def unit(m, c, dp, dq, half=None):
        dy, dx = (dq, dp) if m == 0 else (dp, dq)
        yy, xx = lax.rem(y + dy + SIDE, SIDE), lax.rem(x + dx + SIDE, SIDE)
        return gathered.at[m, core, yy, xx, part_of(c, half)]

    def neighbour(m, axis, sign):
        along_x = (axis == "p") == (m == 0)
        return chan_of(y, x + sign, core) if along_x else chan_of(y + sign, x, core)

    slots = {}
    for side in (-1, 1):
        for dp in (0, -1, 1, 2):
            for kind in (None, 1):
                slots[("q", side, dp, kind)] = len(slots)
    for side in (-1, 1, 2):
        slots[("p", side, 0, None)] = len(slots)
    for dp in (0, -1, 1, 2):
        slots[("q", 2, dp, None)] = len(slots)

    def copy_of(m, c, dp, dq, axis, side, half, to):
        slot = slots[(axis, side, dp if axis == "q" else 0, None if half is None else 1)]
        ref = unit(m, c, dp, dq, half)
        return pltpu.make_async_remote_copy(
            src_ref=ref, dst_ref=ref, send_sem=ici_send.at[m, 0 if axis == "p" else 1],
            recv_sem=ici_recv.at[m, c, slot],
            device_id={"chan": neighbour(m, axis, to)}, device_id_type=MESH,
        )

    def hand(m, c, dp, dq, axis, sign, half=None):
        copy_of(m, c, dp, dq, axis, sign if sign == 2 else -sign, half, sign).start()

    def arrive(m, c, dp, dq, axis, side, half=None):
        copy_of(m, c, dp, dq, axis, side, half, side).wait_recv()

    def share(m, c, dp, dq):
        ref = unit(m, c, dp, dq)
        pltpu.make_async_remote_copy(
            src_ref=ref, dst_ref=ref, send_sem=sib_send.at[m], recv_sem=sib_recv.at[m],
            device_id={"chan": sibling}, device_id_type=MESH,
        ).start()

    def own(c):
        for m in range(2):
            for sign in (2, 1, -1):
                hand(m, c, 0, 0, "p", sign)
        for m in range(2):
            to_q(m, c, 0)
        for m in range(2):
            share(m, c, 0, 0)

    def to_q(m, c, dp):
        for sign in (2, 1, -1) if STRAIGHT[c] else (1, -1):
            hand(m, c, dp, 0, "q", sign)

    def across(c, dp):
        for m in range(2):
            arrive(m, c, dp, 0, "p", dp)
            to_q(m, c, dp)
            share(m, c, dp, 0)

    def first_q(c, dp):
        for side in (-1, 1):
            for m in range(2):
                arrive(m, c, dp, side, "q", side)
                if not STRAIGHT[c]:
                    hand(m, c, dp, side, "q", -side, half=0 if side < 0 else 1)
                share(m, c, dp, side)

    def second_q(c, dp):
        for m in range(2):
            if STRAIGHT[c]:
                arrive(m, c, dp, 2, "q", 2)
            else:
                arrive(m, c, dp, 2, "q", -1, half=0)
                arrive(m, c, dp, 2, "q", 1, half=1)
            share(m, c, dp, 2)

    def stage(c, k):
        if k == 0:
            collect(c)
            own(c)
        elif k == 1:
            for dp in (-1, 1, 2):
                across(c, dp)
        elif k == 2:
            first_q(c, 0)
        elif k == 3:
            for dp in (-1, 1, 2):
                first_q(c, dp)
        else:
            for dp in (0, -1, 1, 2):
                second_q(c, dp)

    def transpose_own():
        row = lax.broadcasted_iota(jnp.int32, (DEPTH, CH), 0)
        for b in range(GROUP):
            m, i = b // 2, b % 2
            rows = jnp.concatenate([gathered[m, core, y, x, part, :] for part in depth_of(i)], axis=0).astype(F32)
            turned = jnp.where(lax.rem(row, 2) == 0, pltpu.roll(rows, DEPTH - 1, 0), -pltpu.roll(rows, 1, 0))
            own_t[b, :CH, :] = rows.T.astype(BF16)
            own_t[b, CH:, :] = turned.T.astype(BF16)

    for c, k in PLAN:
        stage(c, k)
        if (c, k) == (0, 4):
            transpose_own()

    halo.wait_send()
    for copy in sent:
        copy.wait_send()
    for m in range(2):
        for axis, all_sent in ((0, gathered.at[m, core, 0, pl.ds(0, 3)]), (1, gathered.at[m, core, pl.ds(0, 3)])):
            pltpu.make_async_remote_copy(
                src_ref=all_sent, dst_ref=all_sent, send_sem=ici_send.at[m, axis], recv_sem=ici_recv.at[m, 0, 0],
                device_id={"chan": sibling}, device_id_type=MESH,
            ).wait_send()
        shared = pltpu.make_async_remote_copy(
            src_ref=gathered.at[m, core], dst_ref=gathered.at[m, 1 - core],
            send_sem=sib_send.at[m], recv_sem=sib_recv.at[m],
            device_id={"chan": sibling}, device_id_type=MESH,
        )
        shared.wait_send()
        shared.wait_recv()


def product_kernel(gathered, own_t, out, held, sems):
    wide = CORES * CH
    copies = []
    for b in range(GROUP):
        m, i = b // 2, b % 2
        for place in range(SIDE * SIDE):
            yy, xx = place // SIDE, place % SIDE
            right = jnp.concatenate(
                [jnp.concatenate([gathered[m, c, yy, xx, part, :] for part in depth_of(i)], axis=0) for c in range(CORES)],
                axis=1,
            )
            product = jnp.dot(own_t[b], right, preferred_element_type=F32) * (1.0 / FRAMES)
            product = product.astype(BF16)
            columns = slice(place * wide, place * wide + wide)
            held[b, 0, :, columns] = product[:CH]
            held[b, 1, :, columns] = product[CH:]
        copies.append(pltpu.make_async_copy(held.at[b], out.at[b], sems.at[b]))
        copies[-1].start()
    for copy in copies:
        copy.wait()


def local(raw_traces):
    any_space = pl.BlockSpec(memory_space=pl.ANY)
    vmem = pl.BlockSpec(memory_space=pltpu.VMEM)
    gathered, own_t = pl.pallas_call(
        gather_kernel,
        out_shape=(
            pltpu.VMEM((2, CORES, SIDE, SIDE, UNIT, CH), BF16),
            pltpu.VMEM((GROUP, 2 * CH, DEPTH), BF16),
        ),
        in_specs=[any_space] * 2,
        out_specs=(vmem, vmem),
        scratch_shapes=[
            pltpu.VMEM((PIECES * HOP, CH), BF16),
            pltpu.VMEM((4 * SPAN, HOP), BF16),
            pltpu.VMEM((HOP, CH), F32),
            pltpu.VMEM((PIECES, 2 * SPAN, CH), F32),
            pltpu.VMEM((2 * SPAN, CH), F32),
            pltpu.VMEM((2 * SPAN, CH), F32),
            pltpu.VMEM((ROWS * SPAN, CH), F32),
            pltpu.VMEM((PARTS, TM - 1, GROUP * PART, CH), BF16),
            pltpu.VMEM((PARTS, TM, GROUP * PART, CH), BF16),
            pltpu.SemaphoreType.DMA((6,)),
            pltpu.SemaphoreType.DMA((2,)),
            pltpu.SemaphoreType.DMA((PARTS, TM - 1)),
            pltpu.SemaphoreType.DMA((PARTS, TM)),
            pltpu.SemaphoreType.DMA((2, 2)),
            pltpu.SemaphoreType.DMA((2, PARTS, 23)),
            pltpu.SemaphoreType.DMA((2,)),
            pltpu.SemaphoreType.DMA((2,)),
        ],
        compiler_params=pltpu.CompilerParams(
            collective_id=0, has_side_effects=True, vmem_limit_bytes=24 * 1024 * 1024
        ),
    )(*(pltpu.with_memory_space_constraint(a, pltpu.HBM) for a in (raw_traces, spectral_table())))
    return pl.pallas_call(
        product_kernel,
        out_shape=jax.ShapeDtypeStruct((GROUP, 2, CH, SIDE * SIDE * CORES * CH), BF16),
        in_specs=[vmem, vmem],
        out_specs=any_space,
        scratch_shapes=[
            pltpu.VMEM((GROUP, 2, CH, SIDE * SIDE * CORES * CH), BF16),
            pltpu.SemaphoreType.DMA((GROUP,)),
        ],
        compiler_params=pltpu.CompilerParams(vmem_limit_bytes=24 * 1024 * 1024),
    )(
        pltpu.with_memory_space_constraint(gathered, pltpu.VMEM),
        pltpu.with_memory_space_constraint(own_t, pltpu.VMEM),
    )


def solution(mesh):
    return jax.shard_map(
        local, mesh=mesh, in_specs=(P("tm", "chan"),), out_specs=P("tm", None, "chan", None), check_vma=False
    )
```

```python
import functools
import math

import jax
import jax.numpy as jnp
import numpy as np
from jax import lax
from jax.experimental import pallas as pl
from jax.experimental.pallas import tpu as pltpu
from jax.sharding import PartitionSpec as P

NFFT = 1024
HOP = NFFT // 2
NBINS = 32
SMOOTH = 4
BAND_START = 64
SPAN = NBINS + 2 * SMOOTH
FLOOR = 0.125 * math.sqrt(NFFT)
TM = 8
SIDE = 4
CORES = 2
CH = 128
PIECES = 12
FRAMES = TM * PIECES
GROUP = NBINS // TM
ROWS = 2 * PIECES
FIRST = 16
PARTS = (FIRST, ROWS - FIRST)
LINES = tuple(part * TM for part in PARTS)
STARTS = tuple(2 * sum(LINES[:c]) for c in range(len(LINES)))
UNIT = 2 * sum(LINES)
DEPTH = sum(LINES)
PLAN = tuple((c, stage) for stage in range(5) for c in range(len(PARTS)))
MESH = pl.DeviceIdType.MESH
F32 = jnp.float32
BF16 = jnp.bfloat16


def spectral_table():
    sample = np.arange(NFFT)
    bins = BAND_START - SMOOTH + np.arange(SPAN)
    angles = (sample[:, None] * bins[None, :] % NFFT).astype(np.float64) * (2.0 * math.pi / NFFT)
    table = np.concatenate([np.cos(angles), -np.sin(angles)], axis=1).astype(np.float32)
    halves = np.concatenate([table[:HOP].T, table[HOP:].T], axis=0)
    return jnp.asarray(halves.astype(BF16))


def fill_taper(taper):
    step = 2.0 * math.pi / NFFT
    sample = lax.broadcasted_iota(jnp.int32, (8, CH), 0).astype(F32) * step
    cosine, sine = 0.5 * jnp.cos(sample), 0.5 * jnp.sin(sample)
    for i in range(HOP // 8):
        angle = 8 * i * step
        taper[8 * i : 8 * i + 8, :] = 0.5 - math.cos(angle) * cosine + math.sin(angle) * sine


def part_of(c, half=None):
    if half is None:
        return pl.ds(STARTS[c], 2 * LINES[c])
    return pl.ds(STARTS[c] + half * LINES[c], LINES[c])


def depth_of(i):
    return [part_of(c, i) for c in range(len(PARTS))]


def whiten(spectra):
    real, imag = spectra[:SPAN], spectra[SPAN:]
    magnitude = jnp.sqrt(real * real + imag * imag)
    two = magnitude + pltpu.roll(magnitude, SPAN - 1, 0)
    four = two + pltpu.roll(two, SPAN - 2, 0)
    eight = four + pltpu.roll(four, SPAN - 4, 0)
    nine = eight + pltpu.roll(magnitude, SPAN - 8, 0)
    factor = 1.0 / jnp.maximum(nine * (1.0 / (2 * SMOOTH + 1)), FLOOR)
    factor = pltpu.roll(factor, SMOOTH, 0)
    return real * factor, imag * factor


def gather_kernel(
    raw_hbm, table_hbm, gathered, own_t,
    raw, table, taper, spec, halo_out, halo_in, white, to_tm, from_tm,
    load_sem, halo_sem, tm_send, tm_recv, ici_send, ici_recv, sib_send, sib_recv,
):
    z = lax.axis_index("tm")
    chan = lax.axis_index("chan")
    core = lax.rem(chan, CORES)
    place = chan // CORES
    y, x = place // SIDE, lax.rem(place, SIDE)

    def chan_of(yy, xx, cc):
        return (lax.rem(yy + SIDE, SIDE) * SIDE + lax.rem(xx + SIDE, SIDE)) * CORES + cc

    sibling = chan_of(y, x, 1 - core)

    chunks = [(0, 2), (2, 4), (6, 6)]
    loads = [pltpu.make_async_copy(table_hbm, table, load_sem.at[0])]
    for i, (first, count) in enumerate(chunks):
        part = pl.ds(first * HOP, count * HOP)
        loads.append(pltpu.make_async_copy(raw_hbm.at[part], raw.at[part], load_sem.at[1 + i]))
    for copy in loads:
        copy.start()

    barrier = pltpu.get_barrier_semaphore()
    for d in range(1, TM):
        pl.semaphore_signal(barrier, inc=1, device_id={"tm": lax.rem(z + d, TM)}, device_id_type=MESH)
    for dy, dx in ((0, 1), (0, -1), (1, 0), (-1, 0), (0, 2), (2, 0)):
        pl.semaphore_signal(barrier, inc=1, device_id={"chan": chan_of(y + dy, x + dx, core)}, device_id_type=MESH)
    pl.semaphore_signal(barrier, inc=1, device_id={"chan": sibling}, device_id_type=MESH)

    def piece(p):
        return raw[pl.ds(p * HOP, HOP), :].astype(F32)

    fill_taper(taper)
    loads[0].wait()
    loads[1].wait()
    halo_out[...] = jnp.dot(
        table[2 * SPAN :, :], (piece(0) * (1.0 - taper[...])).astype(BF16), preferred_element_type=F32
    )
    halo = pltpu.make_async_remote_copy(
        src_ref=halo_out, dst_ref=halo_in, send_sem=halo_sem.at[0], recv_sem=halo_sem.at[1],
        device_id={"tm": lax.rem(z + TM - 1, TM)}, device_id_type=MESH,
    )

    def enter():
        pl.semaphore_wait(barrier, TM - 1 + 7)
        halo.start()

    middle = (z >= 4) & (z <= 6)
    pl.when(middle)(enter)

    def keep(k, spectra):
        real, imag = whiten(spectra)
        white[pl.ds(2 * k * SPAN, SPAN), :] = real
        white[pl.ds((2 * k + 1) * SPAN, SPAN), :] = imag

    def transform(pair):
        a, b = 2 * pair, 2 * pair + 1
        one, two = piece(a), piece(b)
        up = jnp.concatenate([one * taper[...], two * taper[...]], axis=1).astype(BF16)
        first = jnp.dot(table[: 2 * SPAN, :], up, preferred_element_type=F32)
        spec[a] = first[:, :CH]
        spec[b] = first[:, CH:]
        fall = 1.0 - taper[...]
        down = jnp.concatenate([one * fall, two * fall], axis=1).astype(BF16)
        second = jnp.dot(table[2 * SPAN :, :], down, preferred_element_type=F32)
        if a > 0:
            spec[a - 1] = spec[a - 1] + second[:, :CH]
        spec[b - 1] = spec[b - 1] + second[:, CH:]

    order = (4, 3, -3, 2, -2, 1, -1)

    def rows_for(owner, part):
        first = (part * FIRST) * SPAN + SMOOTH + owner * GROUP
        rows = [white[pl.ds(first + b, PARTS[part], stride=SPAN), :] for b in range(GROUP)]
        return jnp.concatenate(rows, axis=0).astype(BF16)

    def exchange(part):
        count = pl.ds(0, GROUP * PARTS[part])
        for i, d in enumerate(order):
            target = lax.rem(z + d + TM, TM)
            to_tm[part, i, count, :] = rows_for(target, part)
            copy = pltpu.make_async_remote_copy(
                src_ref=to_tm.at[part, i, count], dst_ref=from_tm.at[part, z, count],
                send_sem=tm_send.at[part], recv_sem=tm_recv.at[part],
                device_id={"tm": target}, device_id_type=MESH,
            )
            copy.start()
        from_tm[part, z, count, :] = rows_for(z, part)

    def collect(part):
        lines, count = PARTS[part], pl.ds(0, GROUP * PARTS[part])
        ref = from_tm.at[part, pl.ds(0, TM - 1), count]
        pltpu.make_async_remote_copy(
            src_ref=ref, dst_ref=ref, send_sem=tm_send.at[part], recv_sem=tm_recv.at[part],
            device_id={"tm": lax.rem(z + 1, TM)}, device_id_type=MESH,
        ).wait_recv()
        rows = [from_tm[part, source, count, :].astype(F32) for source in range(TM)]
        for b in range(GROUP):
            m, i = b // 2, b % 2
            whole = jnp.concatenate([block[b * lines : (b + 1) * lines] for block in rows], axis=0)
            gathered[m, core, y, x, part_of(part, i), :] = whole.astype(BF16)

    for pair in range(PIECES // 2):
        for i, (first, count) in enumerate(chunks):
            if i > 0 and first == 2 * pair:
                loads[1 + i].wait()
        transform(pair)
        if pair == FIRST // 4:
            for k in range(FIRST // 2):
                keep(k, spec[k])
            pl.when(jnp.logical_not(middle))(enter)
            exchange(0)
    for k in range(FIRST // 2, PIECES - 1):
        keep(k, spec[k])
    halo.wait_recv()
    keep(PIECES - 1, spec[PIECES - 1] + jnp.where(z == TM - 1, 0.0, halo_in[...]))
    exchange(1)

    def unit(m, c, dp, dq, half=None):
        dy, dx = (dq, dp) if m == 0 else (dp, dq)
        yy, xx = lax.rem(y + dy + SIDE, SIDE), lax.rem(x + dx + SIDE, SIDE)
        return gathered.at[m, core, yy, xx, part_of(c, half)]

    def neighbour(m, axis, sign):
        along_x = (axis == "p") == (m == 0)
        return chan_of(y, x + sign, core) if along_x else chan_of(y + sign, x, core)

    def slot_of(axis, dp, half):
        if axis == "p":
            return 1 if dp == 2 else 0
        return (2 if half is None else 5) + abs(dp)

    def hand(m, c, dp, dq, axis, sign, half=None):
        ref = unit(m, c, dp, dq, half)
        pltpu.make_async_remote_copy(
            src_ref=ref, dst_ref=ref, send_sem=ici_send.at[m, 0 if axis == "p" else 1],
            recv_sem=ici_recv.at[c, slot_of(axis, sign if axis == "p" else dp, half)],
            device_id={"chan": neighbour(m, axis, sign)}, device_id_type=MESH,
        ).start()

    def settle(c, axis, dp, units, half=None):
        ref = gathered.at[:, core, 0, pl.ds(0, units), part_of(c)]
        pltpu.make_async_remote_copy(
            src_ref=ref, dst_ref=ref, send_sem=ici_send.at[0, 0], recv_sem=ici_recv.at[c, slot_of(axis, dp, half)],
            device_id={"chan": sibling}, device_id_type=MESH,
        ).wait_recv()

    def share(m, c, dp, dq):
        ref = unit(m, c, dp, dq)
        pltpu.make_async_remote_copy(
            src_ref=ref, dst_ref=ref, send_sem=sib_send.at[m], recv_sem=sib_recv.at[m],
            device_id={"chan": sibling}, device_id_type=MESH,
        ).start()

    def own(c):
        for m in range(2):
            for sign in (2, 1, -1):
                hand(m, c, 0, 0, "p", sign)
        for m in range(2):
            to_q(m, c, 0)
        for m in range(2):
            share(m, c, 0, 0)

    def to_q(m, c, dp):
        for sign in (1, -1):
            hand(m, c, dp, 0, "q", sign)

    def across(c, dps):
        settle(c, "p", dps[0], len(dps))
        for dp in dps:
            for m in range(2):
                to_q(m, c, dp)
                share(m, c, dp, 0)

    def first_q(c, dps):
        settle(c, "q", dps[0], 2 * len(dps))
        for dp in dps:
            for side in (-1, 1):
                for m in range(2):
                    hand(m, c, dp, side, "q", -side, half=0 if side < 0 else 1)
                    share(m, c, dp, side)

    def second_q(c, dps):
        settle(c, "q", dps[0], len(dps), 1)
        for dp in dps:
            for m in range(2):
                share(m, c, dp, 2)

    def stage(c, k):
        if k == 0:
            collect(c)
            own(c)
        elif k == 1:
            across(c, (-1, 1))
            across(c, (2,))
        elif k == 2:
            first_q(c, (0,))
        elif k == 3:
            first_q(c, (-1, 1))
            first_q(c, (2,))
        else:
            second_q(c, (0,))
            second_q(c, (-1, 1))
            second_q(c, (2,))

    def transpose_own():
        row = lax.broadcasted_iota(jnp.int32, (DEPTH, CH), 0)
        for b in range(GROUP):
            m, i = b // 2, b % 2
            rows = jnp.concatenate([gathered[m, core, y, x, part, :] for part in depth_of(i)], axis=0).astype(F32)
            turned = jnp.where(lax.rem(row, 2) == 0, pltpu.roll(rows, DEPTH - 1, 0), -pltpu.roll(rows, 1, 0))
            own_t[b, :CH, :] = rows.T.astype(BF16)
            own_t[b, CH:, :] = turned.T.astype(BF16)

    for c, k in PLAN:
        stage(c, k)
        if (c, k) == (0, 4):
            transpose_own()

    halo.wait_send()
    for part in range(2):
        ref = to_tm.at[part, :, pl.ds(0, GROUP * PARTS[part])]
        pltpu.make_async_remote_copy(
            src_ref=ref, dst_ref=ref, send_sem=tm_send.at[part], recv_sem=tm_recv.at[part],
            device_id={"tm": lax.rem(z + 1, TM)}, device_id_type=MESH,
        ).wait_send()
    for m in range(2):
        for axis, all_sent in ((0, gathered.at[m, core, 0, pl.ds(0, 3)]), (1, gathered.at[m, core, pl.ds(0, 3)])):
            pltpu.make_async_remote_copy(
                src_ref=all_sent, dst_ref=all_sent, send_sem=ici_send.at[m, axis], recv_sem=ici_recv.at[0, 0],
                device_id={"chan": sibling}, device_id_type=MESH,
            ).wait_send()
        shared = pltpu.make_async_remote_copy(
            src_ref=gathered.at[m, core], dst_ref=gathered.at[m, 1 - core],
            send_sem=sib_send.at[m], recv_sem=sib_recv.at[m],
            device_id={"chan": sibling}, device_id_type=MESH,
        )
        shared.wait_send()
        shared.wait_recv()


def product_kernel(gathered, own_t, out, held, sems):
    wide = CORES * CH
    copies = []
    for b in range(GROUP):
        m, i = b // 2, b % 2
        for place in range(SIDE * SIDE):
            yy, xx = place // SIDE, place % SIDE
            right = jnp.concatenate(
                [jnp.concatenate([gathered[m, c, yy, xx, part, :] for part in depth_of(i)], axis=0) for c in range(CORES)],
                axis=1,
            )
            product = jnp.dot(own_t[b], right, preferred_element_type=F32) * (1.0 / FRAMES)
            product = product.astype(BF16)
            columns = slice(place * wide, place * wide + wide)
            held[b, 0, :, columns] = product[:CH]
            held[b, 1, :, columns] = product[CH:]
        copies.append(pltpu.make_async_copy(held.at[b], out.at[b], sems.at[b]))
        copies[-1].start()
    for copy in copies:
        copy.wait()


def local(raw_traces):
    any_space = pl.BlockSpec(memory_space=pl.ANY)
    vmem = pl.BlockSpec(memory_space=pltpu.VMEM)
    gathered, own_t = pl.pallas_call(
        gather_kernel,
        out_shape=(
            pltpu.VMEM((2, CORES, SIDE, SIDE, UNIT, CH), BF16),
            pltpu.VMEM((GROUP, 2 * CH, DEPTH), BF16),
        ),
        in_specs=[any_space] * 2,
        out_specs=(vmem, vmem),
        scratch_shapes=[
            pltpu.VMEM((PIECES * HOP, CH), BF16),
            pltpu.VMEM((4 * SPAN, HOP), BF16),
            pltpu.VMEM((HOP, CH), F32),
            pltpu.VMEM((PIECES, 2 * SPAN, CH), F32),
            pltpu.VMEM((2 * SPAN, CH), F32),
            pltpu.VMEM((2 * SPAN, CH), F32),
            pltpu.VMEM((ROWS * SPAN, CH), F32),
            pltpu.VMEM((2, TM - 1, GROUP * FIRST, CH), BF16),
            pltpu.VMEM((2, TM, GROUP * FIRST, CH), BF16),
            pltpu.SemaphoreType.DMA((4,)),
            pltpu.SemaphoreType.DMA((2,)),
            pltpu.SemaphoreType.DMA((2,)),
            pltpu.SemaphoreType.DMA((len(PARTS),)),
            pltpu.SemaphoreType.DMA((2, 2)),
            pltpu.SemaphoreType.DMA((len(PARTS), 8)),
            pltpu.SemaphoreType.DMA((2,)),
            pltpu.SemaphoreType.DMA((2,)),
        ],
        compiler_params=pltpu.CompilerParams(
            collective_id=0, has_side_effects=True, vmem_limit_bytes=24 * 1024 * 1024
        ),
    )(*(pltpu.with_memory_space_constraint(a, pltpu.HBM) for a in (raw_traces, spectral_table())))
    return pl.pallas_call(
        product_kernel,
        out_shape=jax.ShapeDtypeStruct((GROUP, 2, CH, SIDE * SIDE * CORES * CH), BF16),
        in_specs=[vmem, vmem],
        out_specs=any_space,
        scratch_shapes=[
            pltpu.VMEM((GROUP, 2, CH, SIDE * SIDE * CORES * CH), BF16),
            pltpu.SemaphoreType.DMA((GROUP,)),
        ],
        compiler_params=pltpu.CompilerParams(vmem_limit_bytes=24 * 1024 * 1024),
    )(
        pltpu.with_memory_space_constraint(gathered, pltpu.VMEM),
        pltpu.with_memory_space_constraint(own_t, pltpu.VMEM),
    )


def solution(mesh):
    return jax.shard_map(
        local, mesh=mesh, in_specs=(P("tm", "chan"),), out_specs=P("tm", None, "chan", None), check_vma=False
    )
```

```python
import functools
import math

import jax
import jax.numpy as jnp
import numpy as np
from jax import lax
from jax.experimental import pallas as pl
from jax.experimental.pallas import tpu as pltpu
from jax.sharding import PartitionSpec as P

NFFT = 1024
HOP = NFFT // 2
NBINS = 32
SMOOTH = 4
BAND_START = 64
SPAN = NBINS + 2 * SMOOTH
FLOOR = 0.125 * math.sqrt(NFFT)
TM = 8
SIDE = 4
CORES = 2
CH = 128
PIECES = 12
FRAMES = TM * PIECES
GROUP = NBINS // TM
ROWS = 2 * PIECES
FIRST = 8
PARTS = (8, 8, 8)
LINES = tuple(part * TM for part in PARTS)
STARTS = tuple(2 * sum(LINES[:c]) for c in range(len(LINES)))
UNIT = 2 * sum(LINES)
DEPTH = sum(LINES)
PLAN = tuple((c, stage) for stage in range(5) for c in range(len(PARTS)))
MESH = pl.DeviceIdType.MESH
F32 = jnp.float32
BF16 = jnp.bfloat16


def spectral_table():
    sample = np.arange(NFFT)
    bins = BAND_START - SMOOTH + np.arange(SPAN)
    angles = (sample[:, None] * bins[None, :] % NFFT).astype(np.float64) * (2.0 * math.pi / NFFT)
    table = np.concatenate([np.cos(angles), -np.sin(angles)], axis=1).astype(np.float32)
    halves = np.concatenate([table[:HOP].T, table[HOP:].T], axis=0)
    return jnp.asarray(halves.astype(BF16))


def fill_taper(taper):
    step = 2.0 * math.pi / NFFT
    sample = lax.broadcasted_iota(jnp.int32, (8, CH), 0).astype(F32) * step
    cosine, sine = 0.5 * jnp.cos(sample), 0.5 * jnp.sin(sample)
    for i in range(HOP // 8):
        angle = 8 * i * step
        taper[8 * i : 8 * i + 8, :] = 0.5 - math.cos(angle) * cosine + math.sin(angle) * sine


def part_of(c, half=None):
    if half is None:
        return pl.ds(STARTS[c], 2 * LINES[c])
    return pl.ds(STARTS[c] + half * LINES[c], LINES[c])


def depth_of(i):
    return [part_of(c, i) for c in range(len(PARTS))]


def whiten(spectra):
    real, imag = spectra[:SPAN], spectra[SPAN:]
    magnitude = jnp.sqrt(real * real + imag * imag)
    two = magnitude + pltpu.roll(magnitude, SPAN - 1, 0)
    four = two + pltpu.roll(two, SPAN - 2, 0)
    eight = four + pltpu.roll(four, SPAN - 4, 0)
    nine = eight + pltpu.roll(magnitude, SPAN - 8, 0)
    factor = 1.0 / jnp.maximum(nine * (1.0 / (2 * SMOOTH + 1)), FLOOR)
    factor = pltpu.roll(factor, SMOOTH, 0)
    return real * factor, imag * factor


def gather_kernel(
    raw_hbm, table_hbm, gathered, own_t,
    raw, table, taper, spec, halo_out, halo_in, white, to_tm, from_tm,
    load_sem, halo_sem, tm_send, tm_recv, ici_send, ici_recv, sib_send, sib_recv,
):
    z = lax.axis_index("tm")
    chan = lax.axis_index("chan")
    core = lax.rem(chan, CORES)
    place = chan // CORES
    y, x = place // SIDE, lax.rem(place, SIDE)

    def chan_of(yy, xx, cc):
        return (lax.rem(yy + SIDE, SIDE) * SIDE + lax.rem(xx + SIDE, SIDE)) * CORES + cc

    sibling = chan_of(y, x, 1 - core)

    chunks = [(0, 2), (2, 4), (6, 6)]
    loads = [pltpu.make_async_copy(table_hbm, table, load_sem.at[0])]
    for i, (first, count) in enumerate(chunks):
        part = pl.ds(first * HOP, count * HOP)
        loads.append(pltpu.make_async_copy(raw_hbm.at[part], raw.at[part], load_sem.at[1 + i]))
    for copy in loads:
        copy.start()

    barrier = pltpu.get_barrier_semaphore()
    for d in range(1, TM):
        pl.semaphore_signal(barrier, inc=1, device_id={"tm": lax.rem(z + d, TM)}, device_id_type=MESH)
    for dy, dx in ((0, 1), (0, -1), (1, 0), (-1, 0), (0, 2), (2, 0)):
        pl.semaphore_signal(barrier, inc=1, device_id={"chan": chan_of(y + dy, x + dx, core)}, device_id_type=MESH)
    pl.semaphore_signal(barrier, inc=1, device_id={"chan": sibling}, device_id_type=MESH)

    def piece(p):
        return raw[pl.ds(p * HOP, HOP), :].astype(F32)

    fill_taper(taper)
    loads[0].wait()
    loads[1].wait()
    halo_out[...] = jnp.dot(
        table[2 * SPAN :, :], (piece(0) * (1.0 - taper[...])).astype(BF16), preferred_element_type=F32
    )
    halo = pltpu.make_async_remote_copy(
        src_ref=halo_out, dst_ref=halo_in, send_sem=halo_sem.at[0], recv_sem=halo_sem.at[1],
        device_id={"tm": lax.rem(z + TM - 1, TM)}, device_id_type=MESH,
    )

    def enter():
        pl.semaphore_wait(barrier, TM - 1 + 7)
        halo.start()

    middle = (z >= 4) & (z <= 6)

    def keep(k, spectra):
        real, imag = whiten(spectra)
        white[pl.ds(2 * k * SPAN, SPAN), :] = real
        white[pl.ds((2 * k + 1) * SPAN, SPAN), :] = imag

    def transform(pair):
        a, b = 2 * pair, 2 * pair + 1
        one, two = piece(a), piece(b)
        up = jnp.concatenate([one * taper[...], two * taper[...]], axis=1).astype(BF16)
        first = jnp.dot(table[: 2 * SPAN, :], up, preferred_element_type=F32)
        spec[a] = first[:, :CH]
        spec[b] = first[:, CH:]
        fall = 1.0 - taper[...]
        down = jnp.concatenate([one * fall, two * fall], axis=1).astype(BF16)
        second = jnp.dot(table[2 * SPAN :, :], down, preferred_element_type=F32)
        if a > 0:
            spec[a - 1] = spec[a - 1] + second[:, :CH]
        spec[b - 1] = spec[b - 1] + second[:, CH:]

    order = (4, 3, -3, 2, -2, 1, -1)

    def rows_for(owner, part):
        first = (part * FIRST) * SPAN + SMOOTH + owner * GROUP
        rows = [white[pl.ds(first + b, PARTS[part], stride=SPAN), :] for b in range(GROUP)]
        return jnp.concatenate(rows, axis=0).astype(BF16)

    def exchange(part):
        count = pl.ds(0, GROUP * PARTS[part])
        for i, d in enumerate(order):
            target = lax.rem(z + d + TM, TM)
            to_tm[part, i, count, :] = rows_for(target, part)
            copy = pltpu.make_async_remote_copy(
                src_ref=to_tm.at[part, i, count], dst_ref=from_tm.at[part, z, count],
                send_sem=tm_send.at[part], recv_sem=tm_recv.at[part],
                device_id={"tm": target}, device_id_type=MESH,
            )
            copy.start()
        from_tm[part, z, count, :] = rows_for(z, part)

    def collect(part):
        lines, count = PARTS[part], pl.ds(0, GROUP * PARTS[part])
        ref = from_tm.at[part, pl.ds(0, TM - 1), count]
        pltpu.make_async_remote_copy(
            src_ref=ref, dst_ref=ref, send_sem=tm_send.at[part], recv_sem=tm_recv.at[part],
            device_id={"tm": lax.rem(z + 1, TM)}, device_id_type=MESH,
        ).wait_recv()
        rows = [from_tm[part, source, count, :].astype(F32) for source in range(TM)]
        for b in range(GROUP):
            m, i = b // 2, b % 2
            whole = jnp.concatenate([block[b * lines : (b + 1) * lines] for block in rows], axis=0)
            gathered[m, core, y, x, part_of(part, i), :] = whole.astype(BF16)

    for pair in range(PIECES // 2):
        for i, (first, count) in enumerate(chunks):
            if i > 0 and first == 2 * pair:
                loads[1 + i].wait()
        transform(pair)
        if pair in (2, 4):
            part = pair // 2 - 1
            for k in range(4 * part, 4 * part + 4):
                keep(k, spec[k])
            if part == 0:
                enter()
            exchange(part)
    for k in range(8, PIECES - 1):
        keep(k, spec[k])
    halo.wait_recv()
    keep(PIECES - 1, spec[PIECES - 1] + jnp.where(z == TM - 1, 0.0, halo_in[...]))
    exchange(2)

    def unit(m, c, dp, dq, half=None):
        dy, dx = (dq, dp) if m == 0 else (dp, dq)
        yy, xx = lax.rem(y + dy + SIDE, SIDE), lax.rem(x + dx + SIDE, SIDE)
        return gathered.at[m, core, yy, xx, part_of(c, half)]

    def neighbour(m, axis, sign):
        along_x = (axis == "p") == (m == 0)
        return chan_of(y, x + sign, core) if along_x else chan_of(y + sign, x, core)

    def slot_of(axis, dp, half):
        if axis == "p":
            return 1 if dp == 2 else 0
        return (2 if half is None else 5) + abs(dp)

    def hand(m, c, dp, dq, axis, sign, half=None):
        ref = unit(m, c, dp, dq, half)
        pltpu.make_async_remote_copy(
            src_ref=ref, dst_ref=ref, send_sem=ici_send.at[m, 0 if axis == "p" else 1],
            recv_sem=ici_recv.at[c, slot_of(axis, sign if axis == "p" else dp, half)],
            device_id={"chan": neighbour(m, axis, sign)}, device_id_type=MESH,
        ).start()

    def settle(c, axis, dp, units, half=None):
        ref = gathered.at[:, core, 0, pl.ds(0, units), part_of(c)]
        pltpu.make_async_remote_copy(
            src_ref=ref, dst_ref=ref, send_sem=ici_send.at[0, 0], recv_sem=ici_recv.at[c, slot_of(axis, dp, half)],
            device_id={"chan": sibling}, device_id_type=MESH,
        ).wait_recv()

    def share(m, c, dp, dq):
        ref = unit(m, c, dp, dq)
        pltpu.make_async_remote_copy(
            src_ref=ref, dst_ref=ref, send_sem=sib_send.at[m], recv_sem=sib_recv.at[m],
            device_id={"chan": sibling}, device_id_type=MESH,
        ).start()

    def own(c):
        for m in range(2):
            for sign in (2, 1, -1):
                hand(m, c, 0, 0, "p", sign)
        for m in range(2):
            to_q(m, c, 0)
        for m in range(2):
            share(m, c, 0, 0)

    def to_q(m, c, dp):
        for sign in (1, -1):
            hand(m, c, dp, 0, "q", sign)

    def across(c, dps):
        settle(c, "p", dps[0], len(dps))
        for dp in dps:
            for m in range(2):
                to_q(m, c, dp)
                share(m, c, dp, 0)

    def first_q(c, dps):
        settle(c, "q", dps[0], 2 * len(dps))
        for dp in dps:
            for side in (-1, 1):
                for m in range(2):
                    hand(m, c, dp, side, "q", -side, half=0 if side < 0 else 1)
                    share(m, c, dp, side)

    def second_q(c, dps):
        settle(c, "q", dps[0], len(dps), 1)
        for dp in dps:
            for m in range(2):
                share(m, c, dp, 2)

    def stage(c, k):
        if k == 0:
            collect(c)
            own(c)
        elif k == 1:
            across(c, (-1, 1))
            across(c, (2,))
        elif k == 2:
            first_q(c, (0,))
        elif k == 3:
            first_q(c, (-1, 1))
            first_q(c, (2,))
        else:
            second_q(c, (0,))
            second_q(c, (-1, 1))
            second_q(c, (2,))

    def transpose_own():
        row = lax.broadcasted_iota(jnp.int32, (DEPTH, CH), 0)
        for b in range(GROUP):
            m, i = b // 2, b % 2
            rows = jnp.concatenate([gathered[m, core, y, x, part, :] for part in depth_of(i)], axis=0).astype(F32)
            turned = jnp.where(lax.rem(row, 2) == 0, pltpu.roll(rows, DEPTH - 1, 0), -pltpu.roll(rows, 1, 0))
            own_t[b, :CH, :] = rows.T.astype(BF16)
            own_t[b, CH:, :] = turned.T.astype(BF16)

    for c, k in PLAN:
        stage(c, k)
        if (c, k) == (0, 4):
            transpose_own()

    halo.wait_send()
    for part in range(3):
        ref = to_tm.at[part, :, pl.ds(0, GROUP * PARTS[part])]
        pltpu.make_async_remote_copy(
            src_ref=ref, dst_ref=ref, send_sem=tm_send.at[part], recv_sem=tm_recv.at[part],
            device_id={"tm": lax.rem(z + 1, TM)}, device_id_type=MESH,
        ).wait_send()
    for m in range(2):
        for axis, all_sent in ((0, gathered.at[m, core, 0, pl.ds(0, 3)]), (1, gathered.at[m, core, pl.ds(0, 3)])):
            pltpu.make_async_remote_copy(
                src_ref=all_sent, dst_ref=all_sent, send_sem=ici_send.at[m, axis], recv_sem=ici_recv.at[0, 0],
                device_id={"chan": sibling}, device_id_type=MESH,
            ).wait_send()
        shared = pltpu.make_async_remote_copy(
            src_ref=gathered.at[m, core], dst_ref=gathered.at[m, 1 - core],
            send_sem=sib_send.at[m], recv_sem=sib_recv.at[m],
            device_id={"chan": sibling}, device_id_type=MESH,
        )
        shared.wait_send()
        shared.wait_recv()


def product_kernel(gathered, own_t, out, held, sems):
    wide = CORES * CH
    copies = []
    for b in range(GROUP):
        m, i = b // 2, b % 2
        for place in range(SIDE * SIDE):
            yy, xx = place // SIDE, place % SIDE
            right = jnp.concatenate(
                [jnp.concatenate([gathered[m, c, yy, xx, part, :] for part in depth_of(i)], axis=0) for c in range(CORES)],
                axis=1,
            )
            product = jnp.dot(own_t[b], right, preferred_element_type=F32) * (1.0 / FRAMES)
            product = product.astype(BF16)
            columns = slice(place * wide, place * wide + wide)
            held[b, 0, :, columns] = product[:CH]
            held[b, 1, :, columns] = product[CH:]
        copies.append(pltpu.make_async_copy(held.at[b], out.at[b], sems.at[b]))
        copies[-1].start()
    for copy in copies:
        copy.wait()


def local(raw_traces):
    any_space = pl.BlockSpec(memory_space=pl.ANY)
    vmem = pl.BlockSpec(memory_space=pltpu.VMEM)
    gathered, own_t = pl.pallas_call(
        gather_kernel,
        out_shape=(
            pltpu.VMEM((2, CORES, SIDE, SIDE, UNIT, CH), BF16),
            pltpu.VMEM((GROUP, 2 * CH, DEPTH), BF16),
        ),
        in_specs=[any_space] * 2,
        out_specs=(vmem, vmem),
        scratch_shapes=[
            pltpu.VMEM((PIECES * HOP, CH), BF16),
            pltpu.VMEM((4 * SPAN, HOP), BF16),
            pltpu.VMEM((HOP, CH), F32),
            pltpu.VMEM((PIECES, 2 * SPAN, CH), F32),
            pltpu.VMEM((2 * SPAN, CH), F32),
            pltpu.VMEM((2 * SPAN, CH), F32),
            pltpu.VMEM((ROWS * SPAN, CH), F32),
            pltpu.VMEM((3, TM - 1, GROUP * FIRST, CH), BF16),
            pltpu.VMEM((3, TM, GROUP * FIRST, CH), BF16),
            pltpu.SemaphoreType.DMA((4,)),
            pltpu.SemaphoreType.DMA((2,)),
            pltpu.SemaphoreType.DMA((3,)),
            pltpu.SemaphoreType.DMA((len(PARTS),)),
            pltpu.SemaphoreType.DMA((2, 2)),
            pltpu.SemaphoreType.DMA((len(PARTS), 8)),
            pltpu.SemaphoreType.DMA((2,)),
            pltpu.SemaphoreType.DMA((2,)),
        ],
        compiler_params=pltpu.CompilerParams(
            collective_id=0, has_side_effects=True, vmem_limit_bytes=24 * 1024 * 1024
        ),
    )(*(pltpu.with_memory_space_constraint(a, pltpu.HBM) for a in (raw_traces, spectral_table())))
    return pl.pallas_call(
        product_kernel,
        out_shape=jax.ShapeDtypeStruct((GROUP, 2, CH, SIDE * SIDE * CORES * CH), BF16),
        in_specs=[vmem, vmem],
        out_specs=any_space,
        scratch_shapes=[
            pltpu.VMEM((GROUP, 2, CH, SIDE * SIDE * CORES * CH), BF16),
            pltpu.SemaphoreType.DMA((GROUP,)),
        ],
        compiler_params=pltpu.CompilerParams(vmem_limit_bytes=24 * 1024 * 1024),
    )(
        pltpu.with_memory_space_constraint(gathered, pltpu.VMEM),
        pltpu.with_memory_space_constraint(own_t, pltpu.VMEM),
    )


def solution(mesh):
    return jax.shard_map(
        local, mesh=mesh, in_specs=(P("tm", "chan"),), out_specs=P("tm", None, "chan", None), check_vma=False
    )
```

```python
import functools
import math

import jax
import jax.numpy as jnp
import numpy as np
from jax import lax
from jax.experimental import pallas as pl
from jax.experimental.pallas import tpu as pltpu
from jax.sharding import PartitionSpec as P

NFFT = 1024
HOP = NFFT // 2
NBINS = 32
SMOOTH = 4
BAND_START = 64
SPAN = NBINS + 2 * SMOOTH
FLOOR = 0.125 * math.sqrt(NFFT)
TM = 8
SIDE = 4
CORES = 2
CH = 128
PIECES = 12
FRAMES = TM * PIECES
GROUP = NBINS // TM
ROWS = 2 * PIECES
FIRST = 8
PARTS = (8, 8, 8)
LINES = tuple(part * TM for part in PARTS)
STARTS = tuple(2 * sum(LINES[:c]) for c in range(len(LINES)))
UNIT = 2 * sum(LINES)
DEPTH = sum(LINES)
PLAN = tuple((c, stage) for stage in range(5) for c in range(len(PARTS)))
MESH = pl.DeviceIdType.MESH
F32 = jnp.float32
BF16 = jnp.bfloat16


def spectral_table():
    sample = np.arange(NFFT)
    bins = BAND_START - SMOOTH + np.arange(SPAN)
    angles = (sample[:, None] * bins[None, :] % NFFT).astype(np.float64) * (2.0 * math.pi / NFFT)
    table = np.concatenate([np.cos(angles), -np.sin(angles)], axis=1).astype(np.float32)
    halves = np.concatenate([table[:HOP].T, table[HOP:].T], axis=0)
    return jnp.asarray(halves.astype(BF16))


def fill_taper(taper):
    step = 2.0 * math.pi / NFFT
    sample = lax.broadcasted_iota(jnp.int32, (8, CH), 0).astype(F32) * step
    cosine, sine = 0.5 * jnp.cos(sample), 0.5 * jnp.sin(sample)
    for i in range(HOP // 8):
        angle = 8 * i * step
        taper[8 * i : 8 * i + 8, :] = 0.5 - math.cos(angle) * cosine + math.sin(angle) * sine


def part_of(c, half=None):
    if half is None:
        return pl.ds(STARTS[c], 2 * LINES[c])
    return pl.ds(STARTS[c] + half * LINES[c], LINES[c])


def depth_of(i):
    return [part_of(c, i) for c in range(len(PARTS))]


def whiten(spectra):
    real, imag = spectra[:SPAN], spectra[SPAN:]
    magnitude = jnp.sqrt(real * real + imag * imag)
    two = magnitude + pltpu.roll(magnitude, SPAN - 1, 0)
    four = two + pltpu.roll(two, SPAN - 2, 0)
    eight = four + pltpu.roll(four, SPAN - 4, 0)
    nine = eight + pltpu.roll(magnitude, SPAN - 8, 0)
    factor = 1.0 / jnp.maximum(nine * (1.0 / (2 * SMOOTH + 1)), FLOOR)
    factor = pltpu.roll(factor, SMOOTH, 0)
    return real * factor, imag * factor


def gather_kernel(
    raw_hbm, table_hbm, gathered, own_t, held,
    raw, table, taper, spec, halo_out, halo_in, white, to_tm, from_tm,
    load_sem, halo_sem, tm_send, tm_recv, ici_send, ici_recv, sib_send, sib_recv,
):
    z = lax.axis_index("tm")
    chan = lax.axis_index("chan")
    core = lax.rem(chan, CORES)
    place = chan // CORES
    y, x = place // SIDE, lax.rem(place, SIDE)

    def chan_of(yy, xx, cc):
        return (lax.rem(yy + SIDE, SIDE) * SIDE + lax.rem(xx + SIDE, SIDE)) * CORES + cc

    sibling = chan_of(y, x, 1 - core)

    chunks = [(0, 2), (2, 4), (6, 6)]
    loads = [pltpu.make_async_copy(table_hbm, table, load_sem.at[0])]
    for i, (first, count) in enumerate(chunks):
        part = pl.ds(first * HOP, count * HOP)
        loads.append(pltpu.make_async_copy(raw_hbm.at[part], raw.at[part], load_sem.at[1 + i]))
    barrier = pltpu.get_barrier_semaphore()
    for d in range(1, TM):
        pl.semaphore_signal(barrier, inc=1, device_id={"tm": lax.rem(z + d, TM)}, device_id_type=MESH)
    for dy, dx in ((0, 1), (0, -1), (1, 0), (-1, 0), (0, 2), (2, 0)):
        pl.semaphore_signal(barrier, inc=1, device_id={"chan": chan_of(y + dy, x + dx, core)}, device_id_type=MESH)
    pl.semaphore_signal(barrier, inc=1, device_id={"chan": sibling}, device_id_type=MESH)

    for copy in loads:
        copy.start()

    def piece(p):
        return raw[pl.ds(p * HOP, HOP), :].astype(F32)

    fill_taper(taper)
    loads[0].wait()
    loads[1].wait()
    halo_out[...] = jnp.dot(
        table[2 * SPAN :, :], (piece(0) * (1.0 - taper[...])).astype(BF16), preferred_element_type=F32
    )
    halo = pltpu.make_async_remote_copy(
        src_ref=halo_out, dst_ref=halo_in, send_sem=halo_sem.at[0], recv_sem=halo_sem.at[1],
        device_id={"tm": lax.rem(z + TM - 1, TM)}, device_id_type=MESH,
    )

    def enter():
        pl.semaphore_wait(barrier, TM - 1 + 7)
        halo.start()

    middle = (z >= 4) & (z <= 6)

    def keep(k, spectra):
        real, imag = whiten(spectra)
        white[pl.ds(2 * k * SPAN, SPAN), :] = real
        white[pl.ds((2 * k + 1) * SPAN, SPAN), :] = imag

    def transform(pair):
        a, b = 2 * pair, 2 * pair + 1
        one, two = piece(a), piece(b)
        up = jnp.concatenate([one * taper[...], two * taper[...]], axis=1).astype(BF16)
        first = jnp.dot(table[: 2 * SPAN, :], up, preferred_element_type=F32)
        spec[a] = first[:, :CH]
        spec[b] = first[:, CH:]
        fall = 1.0 - taper[...]
        down = jnp.concatenate([one * fall, two * fall], axis=1).astype(BF16)
        second = jnp.dot(table[2 * SPAN :, :], down, preferred_element_type=F32)
        if a > 0:
            spec[a - 1] = spec[a - 1] + second[:, :CH]
        spec[b - 1] = spec[b - 1] + second[:, CH:]

    order = (4, 3, -3, 2, -2, 1, -1)

    def rows_for(owner, part):
        first = (part * FIRST) * SPAN + SMOOTH + owner * GROUP
        rows = [white[pl.ds(first + b, PARTS[part], stride=SPAN), :] for b in range(GROUP)]
        return jnp.concatenate(rows, axis=0).astype(BF16)

    def exchange(part):
        count = pl.ds(0, GROUP * PARTS[part])
        for i, d in enumerate(order):
            target = lax.rem(z + d + TM, TM)
            to_tm[part, i, count, :] = rows_for(target, part)
            copy = pltpu.make_async_remote_copy(
                src_ref=to_tm.at[part, i, count], dst_ref=from_tm.at[part, z, count],
                send_sem=tm_send.at[part], recv_sem=tm_recv.at[part],
                device_id={"tm": target}, device_id_type=MESH,
            )
            copy.start()
        from_tm[part, z, count, :] = rows_for(z, part)

    def collect(part):
        lines, count = PARTS[part], pl.ds(0, GROUP * PARTS[part])
        ref = from_tm.at[part, pl.ds(0, TM - 1), count]
        pltpu.make_async_remote_copy(
            src_ref=ref, dst_ref=ref, send_sem=tm_send.at[part], recv_sem=tm_recv.at[part],
            device_id={"tm": lax.rem(z + 1, TM)}, device_id_type=MESH,
        ).wait_recv()
        rows = [from_tm[part, source, count, :].astype(F32) for source in range(TM)]
        for b in range(GROUP):
            m, i = b // 2, b % 2
            whole = jnp.concatenate([block[b * lines : (b + 1) * lines] for block in rows], axis=0)
            gathered[m, core, y, x, part_of(part, i), :] = whole.astype(BF16)

    for pair in range(PIECES // 2):
        for i, (first, count) in enumerate(chunks):
            if i > 0 and first == 2 * pair:
                loads[1 + i].wait()
        transform(pair)
        if pair in (2, 4):
            part = pair // 2 - 1
            for k in range(4 * part, 4 * part + 4):
                keep(k, spec[k])
            if part == 0:
                enter()
            exchange(part)
    for k in range(8, PIECES - 1):
        keep(k, spec[k])
    halo.wait_recv()
    keep(PIECES - 1, spec[PIECES - 1] + jnp.where(z == TM - 1, 0.0, halo_in[...]))
    exchange(2)

    def unit(m, c, dp, dq, half=None):
        dy, dx = (dq, dp) if m == 0 else (dp, dq)
        yy, xx = lax.rem(y + dy + SIDE, SIDE), lax.rem(x + dx + SIDE, SIDE)
        return gathered.at[m, core, yy, xx, part_of(c, half)]

    def neighbour(m, axis, sign):
        along_x = (axis == "p") == (m == 0)
        return chan_of(y, x + sign, core) if along_x else chan_of(y + sign, x, core)

    def slot_of(axis, dp, half):
        if axis == "p":
            return 1 if dp == 2 else 0
        return (2 if half is None else 5) + abs(dp)

    def hand(m, c, dp, dq, axis, sign, half=None):
        ref = unit(m, c, dp, dq, half)
        pltpu.make_async_remote_copy(
            src_ref=ref, dst_ref=ref, send_sem=ici_send.at[m, 0 if axis == "p" else 1],
            recv_sem=ici_recv.at[c, slot_of(axis, sign if axis == "p" else dp, half)],
            device_id={"chan": neighbour(m, axis, sign)}, device_id_type=MESH,
        ).start()

    def settle(c, axis, dp, units, half=None):
        ref = gathered.at[:, core, 0, pl.ds(0, units), part_of(c)]
        pltpu.make_async_remote_copy(
            src_ref=ref, dst_ref=ref, send_sem=ici_send.at[0, 0], recv_sem=ici_recv.at[c, slot_of(axis, dp, half)],
            device_id={"chan": sibling}, device_id_type=MESH,
        ).wait_recv()

    def share(m, c, dp, dq):
        ref = unit(m, c, dp, dq)
        pltpu.make_async_remote_copy(
            src_ref=ref, dst_ref=ref, send_sem=sib_send.at[0], recv_sem=sib_recv.at[abs(dq)],
            device_id={"chan": sibling}, device_id_type=MESH,
        ).start()

    def shared(dq):
        ref = gathered.at[:, 1 - core, pl.ds(0, 2 if dq == 1 else 1)]
        pltpu.make_async_remote_copy(
            src_ref=ref, dst_ref=ref, send_sem=sib_send.at[0], recv_sem=sib_recv.at[dq],
            device_id={"chan": sibling}, device_id_type=MESH,
        ).wait_recv()

    def own(c):
        for m in range(2):
            for sign in (2, 1, -1):
                hand(m, c, 0, 0, "p", sign)
        for m in range(2):
            to_q(m, c, 0)
        for m in range(2):
            share(m, c, 0, 0)

    def to_q(m, c, dp):
        for sign in (1, -1):
            hand(m, c, dp, 0, "q", sign)

    def across(c, dps):
        settle(c, "p", dps[0], len(dps))
        for dp in dps:
            for m in range(2):
                to_q(m, c, dp)
                share(m, c, dp, 0)

    def first_q(c, dps):
        settle(c, "q", dps[0], 2 * len(dps))
        for dp in dps:
            for side in (-1, 1):
                for m in range(2):
                    hand(m, c, dp, side, "q", -side, half=0 if side < 0 else 1)
                    share(m, c, dp, side)

    def second_q(c, dps):
        settle(c, "q", dps[0], len(dps), 1)
        for dp in dps:
            for m in range(2):
                share(m, c, dp, 2)

    def stage(c, k):
        if k == 0:
            collect(c)
            own(c)
        elif k == 1:
            across(c, (-1, 1))
            across(c, (2,))
        elif k == 2:
            first_q(c, (0,))
        elif k == 3:
            first_q(c, (-1, 1))
            first_q(c, (2,))
        else:
            second_q(c, (0,))
            second_q(c, (-1, 1))
            second_q(c, (2,))

    def transpose_own():
        row = lax.broadcasted_iota(jnp.int32, (DEPTH, CH), 0)
        for b in range(GROUP):
            m, i = b // 2, b % 2
            rows = jnp.concatenate([gathered[m, core, y, x, part, :] for part in depth_of(i)], axis=0).astype(F32)
            turned = jnp.where(lax.rem(row, 2) == 0, pltpu.roll(rows, DEPTH - 1, 0), -pltpu.roll(rows, 1, 0))
            own_t[b, :CH, :] = rows.T.astype(BF16)
            own_t[b, CH:, :] = turned.T.astype(BF16)

    for c, k in PLAN:
        stage(c, k)
        if (c, k) == (len(PARTS) - 1, 2):
            transpose_own()
        if (c, k) == (len(PARTS) - 1, 3):
            shared(0)
            products(gathered, own_t, held, y, x, 0)
        if (c, k) == (len(PARTS) - 2, 4):
            shared(1)
            products(gathered, own_t, held, y, x, -1)
    products(gathered, own_t, held, y, x, 1)

    halo.wait_send()
    for part in range(3):
        ref = to_tm.at[part, :, pl.ds(0, GROUP * PARTS[part])]
        pltpu.make_async_remote_copy(
            src_ref=ref, dst_ref=ref, send_sem=tm_send.at[part], recv_sem=tm_recv.at[part],
            device_id={"tm": lax.rem(z + 1, TM)}, device_id_type=MESH,
        ).wait_send()
    for m in range(2):
        for axis, all_sent in ((0, gathered.at[m, core, 0, pl.ds(0, 3)]), (1, gathered.at[m, core, pl.ds(0, 3)])):
            pltpu.make_async_remote_copy(
                src_ref=all_sent, dst_ref=all_sent, send_sem=ici_send.at[m, axis], recv_sem=ici_recv.at[0, 0],
                device_id={"chan": sibling}, device_id_type=MESH,
            ).wait_send()
    ref = gathered.at[:, core]
    pltpu.make_async_remote_copy(
        src_ref=ref, dst_ref=ref, send_sem=sib_send.at[0], recv_sem=sib_recv.at[0],
        device_id={"chan": sibling}, device_id_type=MESH,
    ).wait_send()
    shared(2)


def products(gathered, own_t, held, y, x, dq, bins=tuple(range(GROUP))):
    wide = CORES * CH

    for along in range(SIDE):
        for b in bins:
            m, i = b // 2, b % 2
            yy, xx = (lax.rem(y + dq + SIDE, SIDE), along) if m == 0 else (along, lax.rem(x + dq + SIDE, SIDE))
            right = jnp.concatenate(
                [jnp.concatenate([gathered[m, c, yy, xx, part, :] for part in depth_of(i)], axis=0) for c in range(CORES)],
                axis=1,
            )
            product = jnp.dot(own_t[b], right, preferred_element_type=F32) * (1.0 / FRAMES)
            product = product.astype(BF16)
            columns = pl.ds(pl.multiple_of((yy * SIDE + xx) * wide, wide), wide)
            held[b, 0, :, columns] = product[:CH]
            held[b, 1, :, columns] = product[CH:]


def product_kernel(gathered, own_t, most, out, held, sems):
    place = lax.axis_index("chan") // CORES
    y, x = place // SIDE, lax.rem(place, SIDE)
    copies = []
    for b in range(GROUP):
        products(gathered, own_t, held, y, x, 2, (b,))
        copies.append(pltpu.make_async_copy(held.at[b], out.at[b], sems.at[b]))
        copies[-1].start()
    for copy in copies:
        copy.wait()


def local(raw_traces):
    any_space = pl.BlockSpec(memory_space=pl.ANY)
    vmem = pl.BlockSpec(memory_space=pltpu.VMEM)
    result = (GROUP, 2, CH, SIDE * SIDE * CORES * CH)
    gathered, own_t, held = pl.pallas_call(
        gather_kernel,
        out_shape=(
            pltpu.VMEM((2, CORES, SIDE, SIDE, UNIT, CH), BF16),
            pltpu.VMEM((GROUP, 2 * CH, DEPTH), BF16),
            pltpu.VMEM(result, BF16),
        ),
        in_specs=[any_space] * 2,
        out_specs=(vmem, vmem, vmem),
        scratch_shapes=[
            pltpu.VMEM((PIECES * HOP, CH), BF16),
            pltpu.VMEM((4 * SPAN, HOP), BF16),
            pltpu.VMEM((HOP, CH), F32),
            pltpu.VMEM((PIECES, 2 * SPAN, CH), F32),
            pltpu.VMEM((2 * SPAN, CH), F32),
            pltpu.VMEM((2 * SPAN, CH), F32),
            pltpu.VMEM((ROWS * SPAN, CH), F32),
            pltpu.VMEM((3, TM - 1, GROUP * FIRST, CH), BF16),
            pltpu.VMEM((3, TM, GROUP * FIRST, CH), BF16),
            pltpu.SemaphoreType.DMA((4,)),
            pltpu.SemaphoreType.DMA((2,)),
            pltpu.SemaphoreType.DMA((3,)),
            pltpu.SemaphoreType.DMA((len(PARTS),)),
            pltpu.SemaphoreType.DMA((2, 2)),
            pltpu.SemaphoreType.DMA((len(PARTS), 8)),
            pltpu.SemaphoreType.DMA((1,)),
            pltpu.SemaphoreType.DMA((3,)),
        ],
        compiler_params=pltpu.CompilerParams(
            collective_id=0, has_side_effects=True, vmem_limit_bytes=24 * 1024 * 1024
        ),
    )(*(pltpu.with_memory_space_constraint(a, pltpu.HBM) for a in (raw_traces, spectral_table())))
    out, _ = pl.pallas_call(
        product_kernel,
        out_shape=(jax.ShapeDtypeStruct(result, BF16), pltpu.VMEM(result, BF16)),
        in_specs=[vmem] * 3,
        out_specs=(any_space, vmem),
        input_output_aliases={2: 1},
        scratch_shapes=[pltpu.SemaphoreType.DMA((GROUP,))],
        compiler_params=pltpu.CompilerParams(vmem_limit_bytes=24 * 1024 * 1024),
    )(*(pltpu.with_memory_space_constraint(array, pltpu.VMEM) for array in (gathered, own_t, held)))
    return out


def solution(mesh):
    return jax.shard_map(
        local, mesh=mesh, in_specs=(P("tm", "chan"),), out_specs=P("tm", None, "chan", None), check_vma=False
    )
```

```python
import functools
import math

import jax
import jax.numpy as jnp
import numpy as np
from jax import lax
from jax.experimental import pallas as pl
from jax.experimental.pallas import tpu as pltpu
from jax.sharding import PartitionSpec as P

NFFT = 1024
HOP = NFFT // 2
NBINS = 32
SMOOTH = 4
BAND_START = 64
SPAN = NBINS + 2 * SMOOTH
FLOOR = 0.125 * math.sqrt(NFFT)
TM = 8
SIDE = 4
CORES = 2
CH = 128
PIECES = 12
FRAMES = TM * PIECES
GROUP = NBINS // TM
ROWS = 2 * PIECES
FIRST = 8
PARTS = (8, 8, 8)
LINES = tuple(part * TM for part in PARTS)
STARTS = tuple(2 * sum(LINES[:c]) for c in range(len(LINES)))
UNIT = 2 * sum(LINES)
DEPTH = sum(LINES)
PLAN = tuple((c, stage) for stage in range(5) for c in range(len(PARTS)))
MESH = pl.DeviceIdType.MESH
F32 = jnp.float32
BF16 = jnp.bfloat16


def spectral_table():
    sample = np.arange(NFFT)
    bins = BAND_START - SMOOTH + np.arange(SPAN)
    angles = (sample[:, None] * bins[None, :] % NFFT).astype(np.float64) * (2.0 * math.pi / NFFT)
    table = np.concatenate([np.cos(angles), -np.sin(angles)], axis=1).astype(np.float32)
    halves = np.concatenate([table[:HOP].T, table[HOP:].T], axis=0)
    return jnp.asarray(halves.astype(BF16))


def fill_taper(taper):
    step = 2.0 * math.pi / NFFT
    sample = lax.broadcasted_iota(jnp.int32, (8, CH), 0).astype(F32) * step
    cosine, sine = 0.5 * jnp.cos(sample), 0.5 * jnp.sin(sample)
    for i in range(HOP // 8):
        angle = 8 * i * step
        taper[8 * i : 8 * i + 8, :] = 0.5 - math.cos(angle) * cosine + math.sin(angle) * sine


def part_of(c, half=None):
    if half is None:
        return pl.ds(STARTS[c], 2 * LINES[c])
    return pl.ds(STARTS[c] + half * LINES[c], LINES[c])


def depth_of(i):
    return [part_of(c, i) for c in range(len(PARTS))]


def whiten(spectra):
    real, imag = spectra[:SPAN], spectra[SPAN:]
    magnitude = jnp.sqrt(real * real + imag * imag)
    two = magnitude + pltpu.roll(magnitude, SPAN - 1, 0)
    four = two + pltpu.roll(two, SPAN - 2, 0)
    eight = four + pltpu.roll(four, SPAN - 4, 0)
    nine = eight + pltpu.roll(magnitude, SPAN - 8, 0)
    factor = 1.0 / jnp.maximum(nine * (1.0 / (2 * SMOOTH + 1)), FLOOR)
    factor = pltpu.roll(factor, SMOOTH, 0)
    return real * factor, imag * factor


def gather_kernel(
    raw_hbm, table_hbm, gathered, own_t, held,
    raw, table, taper, spec, halo_out, halo_in, white, to_tm, from_tm,
    load_sem, halo_sem, tm_send, tm_recv, ici_send, ici_recv, sib_send, sib_recv,
):
    z = lax.axis_index("tm")
    chan = lax.axis_index("chan")
    core = lax.rem(chan, CORES)
    place = chan // CORES
    y, x = place // SIDE, lax.rem(place, SIDE)

    def chan_of(yy, xx, cc):
        return (lax.rem(yy + SIDE, SIDE) * SIDE + lax.rem(xx + SIDE, SIDE)) * CORES + cc

    sibling = chan_of(y, x, 1 - core)

    chunks = [(0, 2), (2, 4), (6, 6)]
    loads = [pltpu.make_async_copy(table_hbm, table, load_sem.at[0])]
    for i, (first, count) in enumerate(chunks):
        part = pl.ds(first * HOP, count * HOP)
        loads.append(pltpu.make_async_copy(raw_hbm.at[part], raw.at[part], load_sem.at[1 + i]))
    barrier = pltpu.get_barrier_semaphore()
    for d in range(1, TM):
        pl.semaphore_signal(barrier, inc=1, device_id={"tm": lax.rem(z + d, TM)}, device_id_type=MESH)
    for dy, dx in ((0, 1), (0, -1), (1, 0), (-1, 0), (0, 2), (2, 0)):
        pl.semaphore_signal(barrier, inc=1, device_id={"chan": chan_of(y + dy, x + dx, core)}, device_id_type=MESH)
    pl.semaphore_signal(barrier, inc=1, device_id={"chan": sibling}, device_id_type=MESH)

    for copy in loads:
        copy.start()

    def piece(p):
        return raw[pl.ds(p * HOP, HOP), :].astype(F32)

    fill_taper(taper)
    loads[0].wait()
    loads[1].wait()
    halo_out[...] = jnp.dot(
        table[2 * SPAN :, :], (piece(0) * (1.0 - taper[...])).astype(BF16), preferred_element_type=F32
    )
    halo = pltpu.make_async_remote_copy(
        src_ref=halo_out, dst_ref=halo_in, send_sem=halo_sem.at[0], recv_sem=halo_sem.at[1],
        device_id={"tm": lax.rem(z + TM - 1, TM)}, device_id_type=MESH,
    )

    def enter():
        pl.semaphore_wait(barrier, TM - 1 + 7)
        halo.start()

    middle = (z >= 4) & (z <= 6)

    def keep(k, spectra):
        real, imag = whiten(spectra)
        white[pl.ds(2 * k * SPAN, SPAN), :] = real
        white[pl.ds((2 * k + 1) * SPAN, SPAN), :] = imag

    def transform(pair):
        a, b = 2 * pair, 2 * pair + 1
        one, two = piece(a), piece(b)
        up = jnp.concatenate([one * taper[...], two * taper[...]], axis=1).astype(BF16)
        first = jnp.dot(table[: 2 * SPAN, :], up, preferred_element_type=F32)
        spec[a] = first[:, :CH]
        spec[b] = first[:, CH:]
        fall = 1.0 - taper[...]
        down = jnp.concatenate([one * fall, two * fall], axis=1).astype(BF16)
        second = jnp.dot(table[2 * SPAN :, :], down, preferred_element_type=F32)
        if a > 0:
            spec[a - 1] = spec[a - 1] + second[:, :CH]
        spec[b - 1] = spec[b - 1] + second[:, CH:]

    order = (4, 3, -3, 2, -2, 1, -1)

    def rows_for(owner, part):
        first = (part * FIRST) * SPAN + SMOOTH + owner * GROUP
        rows = [white[pl.ds(first + b, PARTS[part], stride=SPAN), :] for b in range(GROUP)]
        return jnp.concatenate(rows, axis=0).astype(BF16)

    def exchange(part):
        count = pl.ds(0, GROUP * PARTS[part])
        for i, d in enumerate(order):
            target = lax.rem(z + d + TM, TM)
            to_tm[part, i, count, :] = rows_for(target, part)
            copy = pltpu.make_async_remote_copy(
                src_ref=to_tm.at[part, i, count], dst_ref=from_tm.at[part, z, count],
                send_sem=tm_send.at[part], recv_sem=tm_recv.at[part],
                device_id={"tm": target}, device_id_type=MESH,
            )
            copy.start()
        from_tm[part, z, count, :] = rows_for(z, part)

    def collect(part):
        lines, count = PARTS[part], pl.ds(0, GROUP * PARTS[part])
        ref = from_tm.at[part, pl.ds(0, TM - 1), count]
        pltpu.make_async_remote_copy(
            src_ref=ref, dst_ref=ref, send_sem=tm_send.at[part], recv_sem=tm_recv.at[part],
            device_id={"tm": lax.rem(z + 1, TM)}, device_id_type=MESH,
        ).wait_recv()
        rows = [from_tm[part, source, count, :].astype(F32) for source in range(TM)]
        for b in range(GROUP):
            m, i = b // 2, b % 2
            whole = jnp.concatenate([block[b * lines : (b + 1) * lines] for block in rows], axis=0)
            gathered[m, core, y, x, part_of(part, i), :] = whole.astype(BF16)

    for pair in range(PIECES // 2):
        for i, (first, count) in enumerate(chunks):
            if i > 0 and first == 2 * pair:
                loads[1 + i].wait()
        transform(pair)
        if pair in (2, 4):
            part = pair // 2 - 1
            for k in range(4 * part, 4 * part + 4):
                keep(k, spec[k])
            if part == 0:
                enter()
            exchange(part)
    for k in range(8, PIECES - 1):
        keep(k, spec[k])
    halo.wait_recv()
    keep(PIECES - 1, spec[PIECES - 1] + jnp.where(z == TM - 1, 0.0, halo_in[...]))
    exchange(2)

    def unit(m, c, dp, dq, half=None):
        dy, dx = (dq, dp) if m == 0 else (dp, dq)
        yy, xx = lax.rem(y + dy + SIDE, SIDE), lax.rem(x + dx + SIDE, SIDE)
        return gathered.at[m, core, yy, xx, part_of(c, half)]

    def neighbour(m, axis, sign):
        along_x = (axis == "p") == (m == 0)
        return chan_of(y, x + sign, core) if along_x else chan_of(y + sign, x, core)

    def slot_of(axis, dp, half):
        if axis == "p":
            return 1 if dp == 2 else 0
        return (2 if half is None else 5) + abs(dp)

    def hand(m, c, dp, dq, axis, sign, half=None):
        ref = unit(m, c, dp, dq, half)
        pltpu.make_async_remote_copy(
            src_ref=ref, dst_ref=ref, send_sem=ici_send.at[m, 0 if axis == "p" else 1],
            recv_sem=ici_recv.at[c, slot_of(axis, sign if axis == "p" else dp, half)],
            device_id={"chan": neighbour(m, axis, sign)}, device_id_type=MESH,
        ).start()

    def settle(c, axis, dp, units, half=None):
        ref = gathered.at[:, core, 0, pl.ds(0, units), part_of(c)]
        pltpu.make_async_remote_copy(
            src_ref=ref, dst_ref=ref, send_sem=ici_send.at[0, 0], recv_sem=ici_recv.at[c, slot_of(axis, dp, half)],
            device_id={"chan": sibling}, device_id_type=MESH,
        ).wait_recv()

    def share(m, c, dp, dq):
        ref = unit(m, c, dp, dq)
        pltpu.make_async_remote_copy(
            src_ref=ref, dst_ref=ref, send_sem=sib_send.at[0], recv_sem=sib_recv.at[abs(dq)],
            device_id={"chan": sibling}, device_id_type=MESH,
        ).start()

    def shared(dq):
        ref = gathered.at[:, 1 - core, pl.ds(0, 2 if dq == 1 else 1)]
        pltpu.make_async_remote_copy(
            src_ref=ref, dst_ref=ref, send_sem=sib_send.at[0], recv_sem=sib_recv.at[dq],
            device_id={"chan": sibling}, device_id_type=MESH,
        ).wait_recv()

    def own(c):
        for m in range(2):
            for sign in (2, 1, -1):
                hand(m, c, 0, 0, "p", sign)
        for m in range(2):
            to_q(m, c, 0)
        for m in range(2):
            share(m, c, 0, 0)

    def to_q(m, c, dp):
        for sign in (1, -1):
            hand(m, c, dp, 0, "q", sign)

    def across(c, dps):
        settle(c, "p", dps[0], len(dps))
        for dp in dps:
            for m in range(2):
                to_q(m, c, dp)
                share(m, c, dp, 0)

    def first_q(c, dps):
        settle(c, "q", dps[0], 2 * len(dps))
        for dp in dps:
            for side in (-1, 1):
                for m in range(2):
                    hand(m, c, dp, side, "q", -side, half=0 if side < 0 else 1)
                    share(m, c, dp, side)

    def second_q(c, dps):
        settle(c, "q", dps[0], len(dps), 1)
        for dp in dps:
            for m in range(2):
                share(m, c, dp, 2)

    def stage(c, k):
        if k == 0:
            collect(c)
            own(c)
        elif k == 1:
            across(c, (-1, 1))
            across(c, (2,))
        elif k == 2:
            first_q(c, (0,))
        elif k == 3:
            first_q(c, (-1, 1))
            first_q(c, (2,))
        else:
            second_q(c, (0,))
            second_q(c, (-1, 1))
            second_q(c, (2,))

    def transpose_own():
        row = lax.broadcasted_iota(jnp.int32, (DEPTH, CH), 0)
        for b in range(GROUP):
            m, i = b // 2, b % 2
            rows = jnp.concatenate([gathered[m, core, y, x, part, :] for part in depth_of(i)], axis=0).astype(F32)
            turned = jnp.where(lax.rem(row, 2) == 0, pltpu.roll(rows, DEPTH - 1, 0), -pltpu.roll(rows, 1, 0))
            own_t[b, :CH, :] = rows.T.astype(BF16)
            own_t[b, CH:, :] = turned.T.astype(BF16)

    for c, k in PLAN:
        stage(c, k)
        if (c, k) == (len(PARTS) - 1, 2):
            transpose_own()
        if (c, k) == (len(PARTS) - 1, 3):
            shared(0)
            products(gathered, own_t, held, y, x, 0)
        if (c, k) == (len(PARTS) - 2, 4):
            shared(1)
            products(gathered, own_t, held, y, x, -1)
    products(gathered, own_t, held, y, x, 1)

    halo.wait_send()
    for part in range(3):
        ref = to_tm.at[part, :, pl.ds(0, GROUP * PARTS[part])]
        pltpu.make_async_remote_copy(
            src_ref=ref, dst_ref=ref, send_sem=tm_send.at[part], recv_sem=tm_recv.at[part],
            device_id={"tm": lax.rem(z + 1, TM)}, device_id_type=MESH,
        ).wait_send()
    for m in range(2):
        for axis, all_sent in ((0, gathered.at[m, core, 0, pl.ds(0, 3)]), (1, gathered.at[m, core, pl.ds(0, 3)])):
            pltpu.make_async_remote_copy(
                src_ref=all_sent, dst_ref=all_sent, send_sem=ici_send.at[m, axis], recv_sem=ici_recv.at[0, 0],
                device_id={"chan": sibling}, device_id_type=MESH,
            ).wait_send()
    ref = gathered.at[:, core]
    pltpu.make_async_remote_copy(
        src_ref=ref, dst_ref=ref, send_sem=sib_send.at[0], recv_sem=sib_recv.at[0],
        device_id={"chan": sibling}, device_id_type=MESH,
    ).wait_send()
    shared(2)


def products(gathered, own_t, held, y, x, dq, bins=tuple(range(GROUP))):
    wide = CORES * CH

    for along in range(SIDE):
        for b in bins:
            m, i = b // 2, b % 2
            yy, xx = (lax.rem(y + dq + SIDE, SIDE), along) if m == 0 else (along, lax.rem(x + dq + SIDE, SIDE))
            right = jnp.concatenate(
                [jnp.concatenate([gathered[m, c, yy, xx, part, :] for part in depth_of(i)], axis=0) for c in range(CORES)],
                axis=1,
            )
            product = jnp.dot(own_t[b], right, preferred_element_type=F32) * (1.0 / FRAMES)
            product = product.astype(BF16)
            columns = pl.ds(pl.multiple_of((yy * SIDE + xx) * wide, wide), wide)
            held[b, 0, :, columns] = product[:CH]
            held[b, 1, :, columns] = product[CH:]


def product_kernel(gathered, own_t, most, out, held, sems):
    place = lax.axis_index("chan") // CORES
    y, x = place // SIDE, lax.rem(place, SIDE)
    copies = []
    for b in range(GROUP):
        products(gathered, own_t, held, y, x, 2, (b,))
        copies.append(pltpu.make_async_copy(held.at[b], out.at[b], sems.at[b]))
        copies[-1].start()
    for copy in copies:
        copy.wait()


def local(raw_traces):
    any_space = pl.BlockSpec(memory_space=pl.ANY)
    vmem = pl.BlockSpec(memory_space=pltpu.VMEM)
    result = (GROUP, 2, CH, SIDE * SIDE * CORES * CH)
    gathered, own_t, held = pl.pallas_call(
        gather_kernel,
        out_shape=(
            pltpu.VMEM((2, CORES, SIDE, SIDE, UNIT, CH), BF16),
            pltpu.VMEM((GROUP, 2 * CH, DEPTH), BF16),
            pltpu.VMEM(result, BF16),
        ),
        in_specs=[any_space] * 2,
        out_specs=(vmem, vmem, vmem),
        scratch_shapes=[
            pltpu.VMEM((PIECES * HOP, CH), BF16),
            pltpu.VMEM((4 * SPAN, HOP), BF16),
            pltpu.VMEM((HOP, CH), F32),
            pltpu.VMEM((PIECES, 2 * SPAN, CH), F32),
            pltpu.VMEM((2 * SPAN, CH), F32),
            pltpu.VMEM((2 * SPAN, CH), F32),
            pltpu.VMEM(((ROWS + 1) * SPAN, CH), F32),
            pltpu.VMEM((3, TM - 1, GROUP * FIRST, CH), BF16),
            pltpu.VMEM((3, TM, GROUP * FIRST, CH), BF16),
            pltpu.SemaphoreType.DMA((4,)),
            pltpu.SemaphoreType.DMA((2,)),
            pltpu.SemaphoreType.DMA((3,)),
            pltpu.SemaphoreType.DMA((len(PARTS),)),
            pltpu.SemaphoreType.DMA((2, 2)),
            pltpu.SemaphoreType.DMA((len(PARTS), 8)),
            pltpu.SemaphoreType.DMA((1,)),
            pltpu.SemaphoreType.DMA((3,)),
        ],
        compiler_params=pltpu.CompilerParams(
            collective_id=0, has_side_effects=True, vmem_limit_bytes=24 * 1024 * 1024
        ),
    )(*(pltpu.with_memory_space_constraint(a, pltpu.HBM) for a in (raw_traces, spectral_table())))
    out, _ = pl.pallas_call(
        product_kernel,
        out_shape=(jax.ShapeDtypeStruct(result, BF16), pltpu.VMEM(result, BF16)),
        in_specs=[vmem] * 3,
        out_specs=(any_space, vmem),
        input_output_aliases={2: 1},
        scratch_shapes=[pltpu.SemaphoreType.DMA((GROUP,))],
        compiler_params=pltpu.CompilerParams(vmem_limit_bytes=24 * 1024 * 1024),
    )(*(pltpu.with_memory_space_constraint(array, pltpu.VMEM) for array in (gathered, own_t, held)))
    return out


def solution(mesh):
    return jax.shard_map(
        local, mesh=mesh, in_specs=(P("tm", "chan"),), out_specs=P("tm", None, "chan", None), check_vma=False
    )
```
